256 devices in a mesh: dp: 8 (over y, core), tm: 32 (over x, z).
Axes of the slice: x: 4, y: 4, z: 8, core: 2. Of those that a mesh axis runs over, the one named last changes fastest.
Arguments:
- waveform: bfloat16 [8, 4096, 256], P('dp', 'tm'), may hold values from -6 to 6
- speaker_ids: int32 [8], P('dp'), may hold values from 0 to 6111
- speaker_table: bfloat16 [6112, 256], replicated, may hold values from 0.099609375 to 1.8984375
- stencil_taps: float32 [3, 256], replicated, may hold values from -3.5 to 3.5
- skip_gain: float32 [256], replicated, may hold values from 0.5 to 1.5
- filters: float32 [4096, 256], P('tm'), may hold values from -0.09375 to 0.09375
- cotangent: bfloat16 [8, 4096, 256], P('dp', 'tm'), may hold values from -6 to 6
Outputs:
- layer_out: float32 [8, 4096, 256], P('dp', 'tm')
- grad_waveform: float32 [8, 4096, 256], P('dp', 'tm')
- filter_grad: float32 [4096, 256], P('tm')
The draws below stay inside these ranges and needn't reach their ends.
All inputs are finite; a program needn't handle non-finite values.
Results may differ from the reference program's by a relative error of at most 0.0003.
Values may be sent and summed in bfloat16 or wider, within the bound.
A program may use at most 64 MiB of HBM per device.

```python
import jax
import jax.numpy as jnp
from jax import lax

C = 256
SPEAKERS = 6112
LENGTH = 4096
CLIPS = 8


def touch_ends(result, key, smallest, high):
    extent = result.shape
    spot = [jax.random.randint(jax.random.fold_in(key, axis), (), 0, extent[axis]) for axis in range(len(extent))]
    result = result.at[tuple(spot)].set(smallest)
    longest = extent.index(max(extent))
    spot[longest] = (spot[longest] + 1) % extent[longest]
    return result.at[tuple(spot)].set(high)


def block_scale(stream_key, shape, pieces, low, largest):
    loudness, own = 1.0, jax.random.fold_in(stream_key, 6)
    for axis_at, blocks in pieces:
        steps = jnp.exp(jax.random.uniform(jax.random.fold_in(own, axis_at), (blocks,), jnp.float32, low / len(pieces), largest / len(pieces)))
        loudness = loudness * jnp.repeat(steps, shape[axis_at] // blocks).reshape([-1 if axis == axis_at else 1 for axis in range(len(shape))])
    return loudness


def bell_draw(rng, extent, width, most, split=(), kind=jnp.bfloat16):
    level = block_scale(rng, extent, split, -0.22, 0.18) if split else 1.0
    array = jax.random.normal(rng, extent, jnp.float32) * width * level
    return jnp.minimum(jnp.maximum(array, -most), most).astype(kind)


def setup_inputs(seed: int = 0) -> dict:
    arg_keys = jax.random.split(jax.random.key(seed), 8)
    return {
        "waveform": bell_draw(arg_keys[0], (CLIPS, LENGTH, C), 1.0, 6.0, ((0, 8), (1, 32))),
        "speaker_ids": touch_ends(jax.random.randint(arg_keys[1], (CLIPS,), 0, SPEAKERS), jax.random.fold_in(arg_keys[1], 1), 0, SPEAKERS - 1).astype(jnp.int32),
        "speaker_table": jnp.clip(1.0 + 0.18 * jax.random.normal(arg_keys[2], (SPEAKERS, C), jnp.float32), 0.099609375, 1.8984375).astype(jnp.bfloat16),
        "stencil_taps": bell_draw(arg_keys[3], (3, C), 3 ** -0.5, 3.5, (), jnp.float32),
        "skip_gain": jnp.clip(1.0 + 0.1 * jax.random.normal(arg_keys[4], (C,), jnp.float32), 0.5, 1.5),
        "filters": bell_draw(arg_keys[5], (LENGTH, C), LENGTH ** -0.5, 0.09375, ((0, 32),), jnp.float32),
        "cotangent": bell_draw(arg_keys[6], (CLIPS, LENGTH, C), 1.0, 6.0, ((0, 8), (1, 32))),
    }


def stencil_time(field_data, stencil_taps):
    padded = jnp.pad(field_data, ((1, 1), (0, 0)))
    return stencil_taps[0] * padded[:-2] + stencil_taps[1] * padded[1:-1] + stencil_taps[2] * padded[2:]


def reference(waveform, speaker_ids, speaker_table, stencil_taps, skip_gain, filters, cotangent):
    filter_spectrum = jnp.fft.fft(filters, axis=0)
    speaker_rows = speaker_table[speaker_ids].astype(jnp.float32)

    def one_clip(running, inputs):
        clip_data, speaker_row, grad_out = inputs
        value_field = stencil_time(clip_data.astype(jnp.float32), stencil_taps) * speaker_row[None, :]
        value_spectrum = jnp.fft.fft(value_field, axis=0)
        convolved = jnp.real(jnp.fft.ifft(value_spectrum * filter_spectrum, axis=0))
        layer_out = (convolved + skip_gain * value_field).astype(jnp.float32)
        grad_field = grad_out.astype(jnp.float32)
        grad_spectrum = jnp.fft.fft(grad_field, axis=0)
        grad_value = jnp.real(jnp.fft.ifft(grad_spectrum * jnp.conj(filter_spectrum), axis=0)) + skip_gain * grad_field
        filter_term = jnp.conj(value_spectrum) * grad_spectrum
        grad_mid = grad_value * speaker_row[None, :]
        grad_waveform = stencil_time(grad_mid, stencil_taps[::-1]).astype(jnp.float32)
        running = (running[0] + jnp.real(filter_term), running[1] + jnp.imag(filter_term))
        return running, (layer_out, grad_waveform)

    start = (jnp.zeros((LENGTH, C), jnp.float32), jnp.zeros((LENGTH, C), jnp.float32))
    running, outputs = lax.scan(one_clip, start, (waveform, speaker_rows, cotangent))
    total = running[0] + 1j * running[1]
    filter_grad = jnp.real(jnp.fft.ifft(total, axis=0)).astype(jnp.float32)
    return outputs[0], outputs[1], filter_grad
```

```python
import functools
import math

import jax
import jax.numpy as jnp
import ml_dtypes
import numpy as np
from jax import lax
from jax.experimental import pallas as pl
from jax.experimental.pallas import tpu as pltpu
from jax.sharding import PartitionSpec as P

MESH = pl.DeviceIdType.MESH
F32 = jnp.float32
BF16 = jnp.bfloat16
PACK = 8
ROWS16 = 16


def halves(array):
    high = array.astype(ml_dtypes.bfloat16)
    low = (array - high.astype(np.float64)).astype(ml_dtypes.bfloat16)
    return high, low


def make_tables(blocks, samples):
    total = blocks * samples
    index = np.arange(blocks)
    angle = 2.0 * math.pi / blocks * (np.outer(index, index) % blocks)
    spread = np.eye(PACK)
    left = np.concatenate([np.kron(np.cos(angle), spread), -np.kron(np.sin(angle), spread)])
    inner = np.arange(samples)
    angle = 2.0 * math.pi / samples * (np.outer(inner, inner) % samples)
    right = np.block([[np.cos(angle), -np.sin(angle)], [np.sin(angle), np.cos(angle)]])
    turn = 2.0 * math.pi / total * np.outer(index, inner)
    turn = np.repeat(turn, PACK, axis=0)
    return (
        *halves(left),
        *halves(right),
        np.cos(turn).astype(np.float32),
        np.sin(turn).astype(np.float32),
    )


def split(array):
    high = array.astype(BF16)
    return high, (array - high.astype(F32)).astype(BF16)


def dot(a, b):
    return jnp.dot(a, b, preferred_element_type=F32)


def stencil(field, taps):
    lanes = field.shape[2]
    lane = lax.broadcasted_iota(jnp.int32, field.shape, 2)
    edge = jnp.zeros((1,) + field.shape[1:], F32)
    turned = pltpu.roll(field, 1, 2)
    before = jnp.where(lane == 0, jnp.concatenate([edge, turned[:-1]], axis=0), turned)
    turned = pltpu.roll(field, lanes - 1, 2)
    after = jnp.where(lane == lanes - 1, jnp.concatenate([turned[1:], edge], axis=0), turned)
    return taps[0] * before + taps[1] * field + taps[2] * after


def kernel(
    tm_size,
    dp_size,
    ids_ref,
    wave_ref,
    cot_ref,
    filt_ref,
    taps_ref,
    gain_ref,
    speakers_hbm,
    lh_hbm,
    ll_hbm,
    rh_hbm,
    rl_hbm,
    tc_hbm,
    ts_hbm,
    layer_ref,
    gradw_ref,
    fgrad_ref,
    speakers,
    lh,
    ll,
    rh,
    rl,
    tc,
    ts,
    send_a,
    recv_a,
    send_f,
    recv_f,
    send_c,
    recv_c,
    send_r,
    recv_r,
    send_g,
    recv_g,
    local_sem,
    send_sem,
    recv_sem,
):
    dp = lax.axis_index("dp")
    tm = lax.axis_index("tm")
    per = tm_size // dp_size
    samples = wave_ref.shape[0]
    channels = wave_ref.shape[1]
    rows = tm_size * PACK

    barrier = pltpu.get_barrier_semaphore()

    @pl.loop(1, tm_size)
    def _(step):
        pl.semaphore_signal(
            barrier, inc=1, device_id=(dp, lax.rem(tm + step, tm_size)), device_id_type=MESH
        )

    @pl.loop(1, dp_size)
    def _(step):
        pl.semaphore_signal(
            barrier, inc=1, device_id=(lax.rem(dp + step, dp_size), tm), device_id_type=MESH
        )

    loads = [
        pltpu.make_async_copy(source, target, local_sem.at[place])
        for place, (source, target) in enumerate(
            [
                (lh_hbm, lh),
                (ll_hbm, ll),
                (rh_hbm, rh),
                (rl_hbm, rl),
                (tc_hbm, tc),
                (ts_hbm, ts),
                (speakers_hbm, speakers),
            ]
        )
    ]
    for load in loads:
        load.start()

    wave_t = wave_ref[...].astype(F32).T.reshape(tm_size, PACK, samples)
    cot_t = cot_ref[...].astype(F32).T.reshape(tm_size, PACK, samples)
    send_a[...] = jnp.concatenate([wave_t, cot_t], axis=1).astype(BF16)
    send_f[...] = filt_ref[...].T.reshape(tm_size, PACK, samples)

    def exchange(source, target, which):
        @pl.loop(1, tm_size)
        def _(step):
            peer = lax.rem(tm + step, tm_size)
            pltpu.make_async_remote_copy(
                src_ref=source.at[peer],
                dst_ref=target.at[tm],
                send_sem=send_sem.at[which],
                recv_sem=recv_sem.at[which],
                device_id=(dp, peer),
                device_id_type=MESH,
            ).start()

        target[tm] = source[tm]

    def wait_bytes(like, sem):
        pltpu.make_async_copy(like, like, sem).wait()

    pl.semaphore_wait(barrier, tm_size - 1 + dp_size - 1)
    exchange(send_a, recv_a, 0)
    exchange(send_f, recv_f, 1)

    for load in loads:
        load.wait()
    lane = lax.broadcasted_iota(jnp.int32, (PACK, channels), 1)
    row = lax.broadcasted_iota(jnp.int32, (PACK, channels), 0)
    mine = lane == tm * PACK + row

    def column(vector):
        return jnp.sum(jnp.where(mine, vector, 0.0), axis=1, keepdims=True)

    speaker = ids_ref[0]
    group = speakers[lax.div(speaker, ROWS16)]
    picked = lax.broadcasted_iota(jnp.int32, (ROWS16, channels), 0) == lax.rem(speaker, ROWS16)
    speaker_row = jnp.sum(jnp.where(picked, group.astype(F32), 0.0), axis=0, keepdims=True)
    scale = column(speaker_row)
    taps = [column(taps_ref[place : place + 1, :]) for place in range(3)]
    gain = column(gain_ref[...])

    def left_mix(field):
        high, low = split(field)
        return dot(lh[...], high) + (dot(ll[...], high) + dot(lh[...], low))

    def right_mix(field):
        high, low = split(field)
        return dot(high, rh[...]) + (dot(high, rl[...]) + dot(low, rh[...]))

    def twiddle(real, imag):
        return real * tc[...] + imag * ts[...], imag * tc[...] - real * ts[...]

    def forward(fields):
        mixed = left_mix(jnp.concatenate(fields, axis=1))
        turned = []
        for place in range(len(fields)):
            at = slice(place * samples, (place + 1) * samples)
            turned.append(jnp.concatenate(twiddle(mixed[:rows, at], mixed[rows:, at]), axis=1))
        result = right_mix(jnp.concatenate(turned, axis=0))
        return [
            (
                result[place * rows : (place + 1) * rows, :samples],
                result[place * rows : (place + 1) * rows, samples:],
            )
            for place in range(len(fields))
        ]

    def to_blocks(field):
        return field.reshape(tm_size, PACK, samples)

    wait_bytes(recv_a.at[pl.ds(0, tm_size - 1)], recv_sem.at[0])
    both = recv_a[...].astype(F32)
    value = stencil(both[:, :PACK], taps) * scale
    grad = both[:, PACK:]
    (vr, vi), (gr, gi) = forward([value.reshape(rows, samples), grad.reshape(rows, samples)])

    inverse_scale = 1.0 / (tm_size * samples)
    term_r = (vr * gr + vi * gi) * inverse_scale
    term_i = (vr * gi - vi * gr) * inverse_scale
    inner = right_mix(jnp.concatenate([term_r, -term_i], axis=1))
    inner_r, inner_i = twiddle(inner[:, :samples], inner[:, samples:])
    high_r, low_r = split(inner_r)
    high_i, low_i = split(inner_i)
    partial = (
        dot(lh[:rows, :], high_r)
        + dot(ll[:rows, :], high_r)
        + dot(lh[:rows, :], low_r)
        - dot(lh[rows:, :], high_i)
        - dot(ll[rows:, :], high_i)
        - dot(lh[rows:, :], low_i)
    )
    send_r[...] = partial.reshape(dp_size, per * PACK, samples)

    @pl.loop(1, dp_size)
    def _(step):
        peer = lax.rem(dp + step, dp_size)
        pltpu.make_async_remote_copy(
            src_ref=send_r.at[peer],
            dst_ref=recv_r.at[dp],
            send_sem=send_sem.at[2],
            recv_sem=recv_sem.at[2],
            device_id=(peer, tm),
            device_id_type=MESH,
        ).start()

    recv_r[dp] = send_r[dp]

    wait_bytes(recv_f.at[pl.ds(0, tm_size - 1)], recv_sem.at[1])
    ((fr, fi),) = forward([recv_f[...].reshape(rows, samples)])
    fr = fr * inverse_scale
    fi = fi * inverse_scale
    pr = vr * fr - vi * fi
    pi = vr * fi + vi * fr
    qr = gr * fr + gi * fi
    qi = gi * fr - gr * fi
    inner = right_mix(jnp.concatenate([pr - qi, -(pi + qr)], axis=1))
    inner = jnp.concatenate(twiddle(inner[:, :samples], inner[:, samples:]), axis=1)
    mixed = left_mix(inner)
    convolved = mixed[:rows, :samples] - mixed[rows:, samples:]
    correlated = -mixed[rows:, :samples] - mixed[:rows, samples:]

    layer = to_blocks(convolved) + gain * value
    middle = (to_blocks(correlated) + gain * grad) * scale
    send_c[...] = jnp.concatenate([layer, stencil(middle, taps[::-1])], axis=1)
    exchange(send_c, recv_c, 3)

    wait_bytes(recv_r.at[pl.ds(0, dp_size - 1)], recv_sem.at[2])
    total = recv_r[0]
    for place in range(1, dp_size):
        total = total + recv_r[place]
    send_g[...] = total.reshape(per, PACK, samples)
    own = tm // per == dp

    @pl.loop(0, tm_size)
    def _(step):
        place = step // dp_size
        peer_dp = lax.rem(dp + step, dp_size)
        peer_tm = dp * per + place
        itself = (peer_dp == dp) & (peer_tm == tm)

        @pl.when(jnp.logical_not(itself))
        def _():
            pltpu.make_async_remote_copy(
                src_ref=send_g.at[place],
                dst_ref=recv_g.at[tm],
                send_sem=send_sem.at[4],
                recv_sem=recv_sem.at[4],
                device_id=(peer_dp, peer_tm),
                device_id_type=MESH,
            ).start()

        @pl.when(itself)
        def _():
            recv_g[tm] = send_g[place]

    wait_bytes(recv_c.at[pl.ds(0, tm_size - 1)], recv_sem.at[3])
    layer_ref[...] = recv_c[:, :PACK, :].reshape(rows, samples).T
    gradw_ref[...] = recv_c[:, PACK:, :].reshape(rows, samples).T

    @pl.when(own)
    def _():
        wait_bytes(recv_g.at[pl.ds(0, tm_size - 1)], recv_sem.at[4])

    @pl.when(jnp.logical_not(own))
    def _():
        wait_bytes(recv_g, recv_sem.at[4])

    fgrad_ref[...] = recv_g[...].reshape(rows, samples).T

    wait_bytes(send_a.at[pl.ds(0, tm_size - 1)], send_sem.at[0])
    wait_bytes(send_f.at[pl.ds(0, tm_size - 1)], send_sem.at[1])
    wait_bytes(send_r.at[pl.ds(0, dp_size - 1)], send_sem.at[2])
    wait_bytes(send_c.at[pl.ds(0, tm_size - 1)], send_sem.at[3])

    @pl.when(own)
    def _():
        wait_bytes(recv_g.at[pl.ds(0, tm_size - 1)], send_sem.at[4])

    @pl.when(jnp.logical_not(own))
    def _():
        wait_bytes(recv_g, send_sem.at[4])


def local(waveform, speaker_ids, speaker_table, stencil_taps, skip_gain, filters, cotangent):
    tm_size, dp_size = lax.axis_size("tm"), lax.axis_size("dp")
    samples, channels = filters.shape
    per = tm_size // dp_size
    rows = tm_size * PACK
    tables = make_tables(tm_size, samples)
    vmem = pl.BlockSpec(memory_space=pltpu.VMEM)
    anywhere = pl.BlockSpec(memory_space=pl.ANY)
    block = jax.ShapeDtypeStruct((samples, channels), F32)
    layer_out, grad_waveform, filter_grad = pl.pallas_call(
        functools.partial(kernel, tm_size, dp_size),
        out_shape=[block, block, block],
        in_specs=[pl.BlockSpec(memory_space=pltpu.SMEM)] + [vmem] * 5 + [anywhere] * 7,
        out_specs=[vmem] * 3,
        scratch_shapes=[
            pltpu.VMEM((speaker_table.shape[0] // ROWS16, ROWS16, channels), BF16),
            *[pltpu.VMEM(table.shape, table.dtype) for table in tables],
            pltpu.VMEM((tm_size, 2 * PACK, samples), BF16),
            pltpu.VMEM((tm_size, 2 * PACK, samples), BF16),
            pltpu.VMEM((tm_size, PACK, samples), F32),
            pltpu.VMEM((tm_size, PACK, samples), F32),
            pltpu.VMEM((tm_size, 2 * PACK, samples), F32),
            pltpu.VMEM((tm_size, 2 * PACK, samples), F32),
            pltpu.VMEM((dp_size, per * PACK, samples), F32),
            pltpu.VMEM((dp_size, per * PACK, samples), F32),
            pltpu.VMEM((per, PACK, samples), F32),
            pltpu.VMEM((tm_size, PACK, samples), F32),
            pltpu.SemaphoreType.DMA((7,)),
            pltpu.SemaphoreType.DMA((5,)),
            pltpu.SemaphoreType.DMA((5,)),
        ],
        compiler_params=pltpu.CompilerParams(
            collective_id=0, has_side_effects=True, vmem_limit_bytes=40 * 1024 * 1024
        ),
    )(
        speaker_ids,
        waveform[0],
        cotangent[0],
        filters,
        stencil_taps,
        skip_gain[None],
        speaker_table.reshape(-1, ROWS16, channels),
        *[jnp.asarray(table) for table in tables],
    )
    return layer_out[None], grad_waveform[None], filter_grad


def solution(mesh):
    return jax.shard_map(
        local,
        mesh=mesh,
        in_specs=(P("dp", "tm", None), P("dp"), P(), P(), P(), P("tm", None), P("dp", "tm", None)),
        out_specs=(P("dp", "tm", None), P("dp", "tm", None), P("tm", None)),
        check_vma=False,
    )
```

```python
import functools
import math

import jax
import jax.numpy as jnp
import numpy as np
from jax import lax
from jax.experimental import pallas as pl
from jax.experimental.pallas import tpu as pltpu
from jax.sharding import PartitionSpec as P

MESH = pl.DeviceIdType.MESH
F32 = jnp.float32
BF16 = jnp.bfloat16
PACK = 8
ROWS16 = 16


def make_table(blocks, samples):
    total = blocks * samples
    index = np.arange(blocks)
    angle = 2.0 * math.pi / blocks * (np.outer(index, index) % blocks)
    spread = np.eye(PACK)
    left = np.concatenate([np.kron(np.cos(angle), spread), -np.kron(np.sin(angle), spread)])
    inner = np.arange(samples)
    angle = 2.0 * math.pi / samples * (np.outer(inner, inner) % samples)
    right = np.block([[np.cos(angle), -np.sin(angle)], [np.sin(angle), np.cos(angle)]])
    turn = 2.0 * math.pi / total * np.outer(index, inner)
    turn = np.repeat(turn, PACK, axis=0)
    turn = np.concatenate([np.cos(turn), np.sin(turn)], axis=1)
    wide = max(left.shape[1], right.shape[1])
    parts = [np.pad(part, ((0, 0), (0, wide - part.shape[1]))) for part in (left, right, turn)]
    return np.concatenate(parts).astype(np.float32)


def split(array):
    high = array.astype(BF16)
    return high, (array - high.astype(F32)).astype(BF16)


def dot(a, b):
    return jnp.dot(a, b, preferred_element_type=F32)


def far_first(step, size):
    shift = lax.div(step + 1, 2)
    return lax.rem(size + size // 2 + jnp.where(lax.rem(step, 2) == 1, -shift, shift), size)


def stencil(field, taps):
    lanes = field.shape[2]
    lane = lax.broadcasted_iota(jnp.int32, field.shape, 2)
    edge = jnp.zeros((1,) + field.shape[1:], F32)
    turned = pltpu.roll(field, 1, 2)
    before = jnp.where(lane == 0, jnp.concatenate([edge, turned[:-1]], axis=0), turned)
    turned = pltpu.roll(field, lanes - 1, 2)
    after = jnp.where(lane == lanes - 1, jnp.concatenate([turned[1:], edge], axis=0), turned)
    return taps[0] * before + taps[1] * field + taps[2] * after


def kernel(
    tm_size,
    dp_size,
    ids_hbm,
    wave_hbm,
    cot_hbm,
    filt_hbm,
    taps_hbm,
    gain_hbm,
    speakers_hbm,
    table_hbm,
    recv_c,
    recv_g,
    ids,
    wave_ref,
    cot_ref,
    filt_ref,
    taps_ref,
    gain_ref,
    speakers,
    table,
    lh,
    ll,
    rh,
    rl,
    send_a,
    recv_a,
    send_f,
    recv_f,
    send_c,
    send_r,
    recv_r,
    send_g,
    local_sem,
    send_sem,
    recv_sem,
):
    dp = lax.axis_index("dp")
    tm = lax.axis_index("tm")
    per = tm_size // dp_size
    place = lax.div(tm, dp_size)
    column_at = lax.rem(tm, dp_size)
    samples = wave_ref.shape[0]
    channels = wave_ref.shape[1]
    rows = tm_size * PACK

    barrier = pltpu.get_barrier_semaphore()

    @pl.loop(1, tm_size)
    def _(step):
        pl.semaphore_signal(
            barrier, inc=1, device_id=(dp, lax.rem(tm + step, tm_size)), device_id_type=MESH
        )

    @pl.loop(1, dp_size)
    def _(step):
        pl.semaphore_signal(
            barrier, inc=1, device_id=(lax.rem(dp + step, dp_size), tm), device_id_type=MESH
        )

    pairs = [
        (wave_hbm, wave_ref),
        (cot_hbm, cot_ref),
        (filt_hbm, filt_ref),
        (table_hbm, table),
        (taps_hbm, taps_ref),
        (gain_hbm, gain_ref),
        (ids_hbm, ids),
        (speakers_hbm, speakers),
    ]
    loads = [
        pltpu.make_async_copy(source, target, local_sem.at[slot])
        for slot, (source, target) in enumerate(pairs)
    ]

    def wait_bytes(like, sem):
        pltpu.make_async_copy(like, like, sem).wait()

    def exchange(source, target, which):
        @pl.loop(0, tm_size - 1)
        def _(step):
            far = far_first(lax.div(step, per), dp_size)
            across = far_first(lax.rem(step, per), per)
            peer = lax.rem(place + across, per) * dp_size + lax.rem(column_at + far, dp_size)
            pltpu.make_async_remote_copy(
                src_ref=source.at[peer],
                dst_ref=target.at[tm],
                send_sem=send_sem.at[which],
                recv_sem=recv_sem.at[which],
                device_id=(dp, peer),
                device_id_type=MESH,
            ).start()

    def to_blocks(field):
        return field.reshape(tm_size, PACK, samples)

    for load in loads[:3]:
        load.start()
    loads[0].wait()
    wave_t = to_blocks(wave_ref[...].astype(F32).T)
    loads[1].wait()
    cot_t = to_blocks(cot_ref[...].astype(F32).T)
    send_a[...] = jnp.concatenate([wave_t, cot_t], axis=1).astype(BF16)
    pl.semaphore_wait(barrier, tm_size - 1 + dp_size - 1)
    exchange(send_a, recv_a, 0)
    recv_a[tm] = send_a[tm]

    loads[2].wait()
    send_f[...] = to_blocks(filt_ref[...].T)
    exchange(send_f, recv_f, 1)
    recv_f[tm] = send_f[tm]

    for load in loads[3:]:
        load.start()
    for load in loads[3:]:
        load.wait()
    lh[...], ll[...] = split(table[: 2 * rows, :rows])
    rh[...], rl[...] = split(table[2 * rows : 2 * rows + 2 * samples, : 2 * samples])
    tc = table[2 * rows + 2 * samples :, :samples]
    ts = table[2 * rows + 2 * samples :, samples : 2 * samples]
    lane = lax.broadcasted_iota(jnp.int32, (PACK, channels), 1)
    row = lax.broadcasted_iota(jnp.int32, (PACK, channels), 0)
    mine = lane == tm * PACK + row

    def column(vector):
        return jnp.sum(jnp.where(mine, vector, 0.0), axis=1, keepdims=True)

    speaker = ids[0]
    group = speakers[lax.div(speaker, ROWS16)]
    picked = lax.broadcasted_iota(jnp.int32, (ROWS16, channels), 0) == lax.rem(speaker, ROWS16)
    speaker_row = jnp.sum(jnp.where(picked, group.astype(F32), 0.0), axis=0, keepdims=True)
    scale = column(speaker_row)
    taps = [column(taps_ref[place : place + 1, :]) for place in range(3)]
    gain = column(gain_ref[...])

    def left_mix(field):
        high, low = split(field)
        return dot(lh[...], high) + (dot(ll[...], high) + dot(lh[...], low))

    def right_mix(field):
        high, low = split(field)
        return dot(high, rh[...]) + (dot(high, rl[...]) + dot(low, rh[...]))

    def twiddle(real, imag):
        return real * tc + imag * ts, imag * tc - real * ts

    def forward(fields):
        mixed = left_mix(jnp.concatenate(fields, axis=1))
        turned = []
        for place in range(len(fields)):
            at = slice(place * samples, (place + 1) * samples)
            turned.append(jnp.concatenate(twiddle(mixed[:rows, at], mixed[rows:, at]), axis=1))
        result = right_mix(jnp.concatenate(turned, axis=0))
        return [
            (
                result[place * rows : (place + 1) * rows, :samples],
                result[place * rows : (place + 1) * rows, samples:],
            )
            for place in range(len(fields))
        ]

    wait_bytes(recv_a.at[pl.ds(0, tm_size - 1)], recv_sem.at[0])
    both = recv_a[...].astype(F32)
    value = stencil(both[:, :PACK], taps) * scale
    grad = both[:, PACK:]
    (vr, vi), (gr, gi) = forward([value.reshape(rows, samples), grad.reshape(rows, samples)])

    inverse_scale = 1.0 / (tm_size * samples)
    term_r = (vr * gr + vi * gi) * inverse_scale
    term_i = (vr * gi - vi * gr) * inverse_scale
    inner = right_mix(jnp.concatenate([term_r, -term_i], axis=1))
    inner_r, inner_i = twiddle(inner[:, :samples], inner[:, samples:])
    high_r, low_r = split(inner_r)
    high_i, low_i = split(inner_i)
    partial = to_blocks(
        dot(lh[:rows, :], high_r)
        + dot(ll[:rows, :], high_r)
        + dot(lh[:rows, :], low_r)
        - dot(lh[rows:, :], high_i)
        - dot(ll[rows:, :], high_i)
        - dot(lh[rows:, :], low_i)
    )

    for block in range(tm_size):
        line = block // dp_size
        send_r[(block - 2 * line) % dp_size, line] = partial[block]

    @pl.loop(0, dp_size - 1)
    def _(step):
        peer = lax.rem(dp + far_first(step, dp_size), dp_size)
        pltpu.make_async_remote_copy(
            src_ref=send_r.at[peer],
            dst_ref=recv_r.at[dp],
            send_sem=send_sem.at[2],
            recv_sem=recv_sem.at[2],
            device_id=(peer, tm),
            device_id_type=MESH,
        ).start()

    recv_r[dp] = send_r[dp]

    wait_bytes(recv_f.at[pl.ds(0, tm_size - 1)], recv_sem.at[1])
    ((fr, fi),) = forward([recv_f[...].reshape(rows, samples)])
    fr = fr * inverse_scale
    fi = fi * inverse_scale
    pr = vr * fr - vi * fi
    pi = vr * fi + vi * fr
    qr = gr * fr + gi * fi
    qi = gi * fr - gr * fi
    inner = right_mix(jnp.concatenate([pr - qi, -(pi + qr)], axis=1))
    inner = jnp.concatenate(twiddle(inner[:, :samples], inner[:, samples:]), axis=1)
    mixed = left_mix(inner)
    convolved = mixed[:rows, :samples] - mixed[rows:, samples:]
    correlated = -mixed[rows:, :samples] - mixed[:rows, samples:]

    layer = to_blocks(convolved) + gain * value
    middle = (to_blocks(correlated) + gain * grad) * scale
    send_c[...] = jnp.concatenate([layer, stencil(middle, taps[::-1])], axis=1)
    exchange(send_c, recv_c, 3)
    own_c = pltpu.make_async_copy(send_c.at[tm], recv_c.at[tm], local_sem.at[8])
    own_c.start()

    wait_bytes(recv_r.at[pl.ds(0, dp_size - 1)], recv_sem.at[2])
    total = recv_r[0]
    for source in range(1, dp_size):
        total = total + recv_r[source]
    send_g[...] = total
    own = lax.rem(dp + 2 * place, dp_size) == column_at
    own_g = pltpu.make_async_copy(send_g.at[place], recv_g.at[tm], local_sem.at[9])

    @pl.loop(0, tm_size)
    def _(step):
        line = lax.rem(place + far_first(lax.rem(step, per), per), per)
        peer_dp = lax.rem(dp + far_first(lax.div(step, per), dp_size), dp_size)
        peer_tm = line * dp_size + lax.rem(dp + 2 * line, dp_size)

        @pl.when(jnp.logical_not((peer_dp == dp) & (peer_tm == tm)))
        def _():
            pltpu.make_async_remote_copy(
                src_ref=send_g.at[line],
                dst_ref=recv_g.at[tm],
                send_sem=send_sem.at[4],
                recv_sem=recv_sem.at[4],
                device_id=(peer_dp, peer_tm),
                device_id_type=MESH,
            ).start()

    wait_bytes(send_a.at[pl.ds(0, tm_size - 1)], send_sem.at[0])
    wait_bytes(send_f.at[pl.ds(0, tm_size - 1)], send_sem.at[1])
    wait_bytes(send_r.at[pl.ds(0, dp_size - 1)], send_sem.at[2])
    wait_bytes(send_c.at[pl.ds(0, tm_size - 1)], send_sem.at[3])
    own_c.wait()
    wait_bytes(recv_c.at[pl.ds(0, tm_size - 1)], recv_sem.at[3])

    @pl.when(own)
    def _():
        own_g.start()
        own_g.wait()
        wait_bytes(recv_g.at[pl.ds(0, tm_size - 1)], send_sem.at[4])
        wait_bytes(recv_g.at[pl.ds(0, tm_size - 1)], recv_sem.at[4])

    @pl.when(jnp.logical_not(own))
    def _():
        wait_bytes(recv_g, send_sem.at[4])
        wait_bytes(recv_g, recv_sem.at[4])


def turn_back(main_hbm, third_hbm, layer_hbm, gradw_hbm, fgrad_hbm, raw, turned, load_sem, store_sem):
    channels, samples = turned.shape[2], turned.shape[1]
    sources = [main_hbm.at[:, :PACK, :], main_hbm.at[:, PACK:, :], third_hbm]
    targets = [layer_hbm, gradw_hbm, fgrad_hbm]
    loads = [
        pltpu.make_async_copy(sources[place], raw.at[place], load_sem.at[place])
        for place in range(3)
    ]
    stores = [
        pltpu.make_async_copy(turned.at[place], targets[place], store_sem.at[place])
        for place in range(3)
    ]
    for load in loads:
        load.start()
    for place in range(3):
        loads[place].wait()
        turned[place] = raw[place].reshape(channels, samples).T
        stores[place].start()
    for store in stores:
        store.wait()


def local(waveform, speaker_ids, speaker_table, stencil_taps, skip_gain, filters, cotangent):
    tm_size, dp_size = lax.axis_size("tm"), lax.axis_size("dp")
    samples, channels = filters.shape
    per = tm_size // dp_size
    rows = tm_size * PACK
    table = make_table(tm_size, samples)
    anywhere = pl.BlockSpec(memory_space=pl.ANY)
    block = jax.ShapeDtypeStruct((samples, channels), F32)
    main, third = pl.pallas_call(
        functools.partial(kernel, tm_size, dp_size),
        out_shape=[
            jax.ShapeDtypeStruct((tm_size, 2 * PACK, samples), F32),
            jax.ShapeDtypeStruct((tm_size, PACK, samples), F32),
        ],
        in_specs=[anywhere] * 8,
        out_specs=[anywhere] * 2,
        scratch_shapes=[
            pltpu.SMEM((1,), jnp.int32),
            pltpu.VMEM((samples, channels), BF16),
            pltpu.VMEM((samples, channels), BF16),
            pltpu.VMEM((samples, channels), F32),
            pltpu.VMEM(stencil_taps.shape, F32),
            pltpu.VMEM((1, channels), F32),
            pltpu.VMEM((speaker_table.shape[0] // ROWS16, ROWS16, channels), BF16),
            pltpu.VMEM(table.shape, F32),
            pltpu.VMEM((2 * rows, rows), BF16),
            pltpu.VMEM((2 * rows, rows), BF16),
            pltpu.VMEM((2 * samples, 2 * samples), BF16),
            pltpu.VMEM((2 * samples, 2 * samples), BF16),
            pltpu.VMEM((tm_size, 2 * PACK, samples), BF16),
            pltpu.VMEM((tm_size, 2 * PACK, samples), BF16),
            pltpu.VMEM((tm_size, PACK, samples), F32),
            pltpu.VMEM((tm_size, PACK, samples), F32),
            pltpu.VMEM((tm_size, 2 * PACK, samples), F32),
            pltpu.VMEM((dp_size, per, PACK, samples), F32),
            pltpu.VMEM((dp_size, per, PACK, samples), F32),
            pltpu.VMEM((per, PACK, samples), F32),
            pltpu.SemaphoreType.DMA((10,)),
            pltpu.SemaphoreType.DMA((5,)),
            pltpu.SemaphoreType.DMA((5,)),
        ],
        compiler_params=pltpu.CompilerParams(
            collective_id=0, has_side_effects=True, vmem_limit_bytes=62 * 1024 * 1024
        ),
    )(
        speaker_ids,
        waveform[0],
        cotangent[0],
        filters,
        stencil_taps,
        skip_gain[None],
        speaker_table.reshape(-1, ROWS16, channels),
        jnp.asarray(table),
    )
    layer_out, grad_waveform, filter_grad = pl.pallas_call(
        turn_back,
        out_shape=[block, block, block],
        in_specs=[anywhere] * 2,
        out_specs=[anywhere] * 3,
        scratch_shapes=[
            pltpu.VMEM((3, tm_size, PACK, samples), F32),
            pltpu.VMEM((3, samples, channels), F32),
            pltpu.SemaphoreType.DMA((3,)),
            pltpu.SemaphoreType.DMA((3,)),
        ],
        compiler_params=pltpu.CompilerParams(vmem_limit_bytes=62 * 1024 * 1024),
    )(main, third)
    return layer_out[None], grad_waveform[None], filter_grad


def solution(mesh):
    return jax.shard_map(
        local,
        mesh=mesh,
        in_specs=(P("dp", "tm", None), P("dp"), P(), P(), P(), P("tm", None), P("dp", "tm", None)),
        out_specs=(P("dp", "tm", None), P("dp", "tm", None), P("tm", None)),
        check_vma=False,
    )
```

```python
import functools
import math

import jax
import jax.numpy as jnp
import numpy as np
from jax import lax
from jax.experimental import pallas as pl
from jax.experimental.pallas import tpu as pltpu
from jax.sharding import PartitionSpec as P

MESH = pl.DeviceIdType.MESH
F32 = jnp.float32
BF16 = jnp.bfloat16
PACK = 8
ROWS16 = 16


def make_table(blocks, samples):
    total = blocks * samples
    index = np.arange(blocks)
    angle = 2.0 * math.pi / blocks * (np.outer(index, index) % blocks)
    spread = np.eye(PACK)
    left = np.concatenate([np.kron(np.cos(angle), spread), -np.kron(np.sin(angle), spread)])
    inner = np.arange(samples)
    angle = 2.0 * math.pi / samples * (np.outer(inner, inner) % samples)
    right = np.block([[np.cos(angle), -np.sin(angle)], [np.sin(angle), np.cos(angle)]])
    turn = 2.0 * math.pi / total * np.outer(index, inner)
    turn = np.repeat(turn, PACK, axis=0)
    turn = np.concatenate([np.cos(turn), np.sin(turn)], axis=1)
    wide = max(left.shape[1], right.shape[1])
    parts = [np.pad(part, ((0, 0), (0, wide - part.shape[1]))) for part in (left, right, turn)]
    return np.concatenate(parts).astype(np.float32)


def split(array):
    high = array.astype(BF16)
    return high, (array - high.astype(F32)).astype(BF16)


def dot(a, b):
    return jnp.dot(a, b, preferred_element_type=F32)


def far_first(step, size):
    shift = lax.div(step + 1, 2)
    return lax.rem(size + size // 2 + jnp.where(lax.rem(step, 2) == 1, -shift, shift), size)


def stencil(field, taps):
    lanes = field.shape[2]
    lane = lax.broadcasted_iota(jnp.int32, field.shape, 2)
    edge = jnp.zeros((1,) + field.shape[1:], F32)
    turned = pltpu.roll(field, 1, 2)
    before = jnp.where(lane == 0, jnp.concatenate([edge, turned[:-1]], axis=0), turned)
    turned = pltpu.roll(field, lanes - 1, 2)
    after = jnp.where(lane == lanes - 1, jnp.concatenate([turned[1:], edge], axis=0), turned)
    return taps[0] * before + taps[1] * field + taps[2] * after


def kernel(
    tm_size,
    dp_size,
    ids_hbm,
    wave_hbm,
    cot_hbm,
    filt_hbm,
    taps_hbm,
    gain_hbm,
    speakers_hbm,
    table_hbm,
    recv_l,
    recv_w,
    recv_g,
    ids,
    wave_ref,
    cot_ref,
    filt_ref,
    taps_ref,
    gain_ref,
    speakers,
    table,
    lh,
    ll,
    rh,
    rl,
    send_a,
    recv_a,
    send_f,
    recv_f,
    send_l,
    send_w,
    send_r,
    recv_r,
    send_g,
    local_sem,
    send_sem,
    recv_sem,
    plane_sem,
):
    dp = lax.axis_index("dp")
    tm = lax.axis_index("tm")
    per = tm_size // dp_size
    place = lax.div(tm, dp_size)
    column_at = lax.rem(tm, dp_size)
    samples = wave_ref.shape[0]
    channels = wave_ref.shape[1]
    rows = tm_size * PACK

    barrier = pltpu.get_barrier_semaphore()

    def tm_peer(step):
        far = far_first(lax.div(step, per), dp_size)
        across = far_first(lax.rem(step, per), per)
        return lax.rem(place + across, per) * dp_size + lax.rem(column_at + far, dp_size)

    def dp_peer(step):
        return lax.rem(dp + far_first(step, dp_size), dp_size)

    @pl.loop(0, tm_size - 1)
    def _(step):
        pl.semaphore_signal(barrier, inc=1, device_id=(dp, tm_peer(step)), device_id_type=MESH)

    @pl.loop(0, dp_size - 1)
    def _(step):
        pl.semaphore_signal(barrier, inc=1, device_id=(dp_peer(step), tm), device_id_type=MESH)

    pairs = [
        (wave_hbm, wave_ref),
        (cot_hbm, cot_ref),
        (filt_hbm, filt_ref),
        (table_hbm, table),
        (taps_hbm, taps_ref),
        (gain_hbm, gain_ref),
        (ids_hbm, ids),
        (speakers_hbm, speakers),
    ]
    loads = [
        pltpu.make_async_copy(source, target, local_sem.at[slot])
        for slot, (source, target) in enumerate(pairs)
    ]

    def wait_bytes(like, sem):
        pltpu.make_async_copy(like, like, sem).wait()

    def exchange(source, target, which):
        @pl.loop(0, tm_size - 1)
        def _(step):
            peer = tm_peer(step)
            pltpu.make_async_remote_copy(
                src_ref=source.at[peer],
                dst_ref=target.at[tm],
                send_sem=send_sem.at[which],
                recv_sem=recv_sem.at[which],
                device_id=(dp, peer),
                device_id_type=MESH,
            ).start()

    def to_blocks(field):
        return field.reshape(tm_size, PACK, samples)

    for load in loads[:3]:
        load.start()
    loads[0].wait()
    wave_t = to_blocks(wave_ref[...].astype(F32).T)
    loads[1].wait()
    cot_t = to_blocks(cot_ref[...].astype(F32).T)
    send_a[...] = jnp.concatenate([wave_t, cot_t], axis=1).astype(BF16)
    pl.semaphore_wait(barrier, tm_size - 1 + dp_size - 1)
    exchange(send_a, recv_a, 0)
    recv_a[tm] = send_a[tm]

    adder = lax.div(tm, per)

    @pl.when(adder == dp)
    def _():
        @pl.loop(0, dp_size - 1)
        def _(step):
            pl.semaphore_signal(plane_sem, inc=1, device_id=(dp_peer(step), tm), device_id_type=MESH)

    loads[2].wait()
    send_f[...] = to_blocks(filt_ref[...].T)
    exchange(send_f, recv_f, 1)
    recv_f[tm] = send_f[tm]

    for load in loads[3:]:
        load.start()
    for load in loads[3:]:
        load.wait()
    lh[...], ll[...] = split(table[: 2 * rows, :rows])
    rh[...], rl[...] = split(table[2 * rows : 2 * rows + 2 * samples, : 2 * samples])
    tc = table[2 * rows + 2 * samples :, :samples]
    ts = table[2 * rows + 2 * samples :, samples : 2 * samples]
    lane = lax.broadcasted_iota(jnp.int32, (PACK, channels), 1)
    row = lax.broadcasted_iota(jnp.int32, (PACK, channels), 0)
    mine = lane == tm * PACK + row

    def column(vector):
        return jnp.sum(jnp.where(mine, vector, 0.0), axis=1, keepdims=True)

    speaker = ids[0]
    group = speakers[lax.div(speaker, ROWS16)]
    picked = lax.broadcasted_iota(jnp.int32, (ROWS16, channels), 0) == lax.rem(speaker, ROWS16)
    speaker_row = jnp.sum(jnp.where(picked, group.astype(F32), 0.0), axis=0, keepdims=True)
    scale = column(speaker_row)
    taps = [column(taps_ref[place : place + 1, :]) for place in range(3)]
    gain = column(gain_ref[...])

    def left_mix(field):
        high, low = split(field)
        return dot(lh[...], high) + (dot(ll[...], high) + dot(lh[...], low))

    def right_mix(field):
        high, low = split(field)
        return dot(high, rh[...]) + (dot(high, rl[...]) + dot(low, rh[...]))

    def twiddle(real, imag):
        return real * tc + imag * ts, imag * tc - real * ts

    def forward(fields):
        mixed = left_mix(jnp.concatenate(fields, axis=1))
        turned = []
        for place in range(len(fields)):
            at = slice(place * samples, (place + 1) * samples)
            turned.append(jnp.concatenate(twiddle(mixed[:rows, at], mixed[rows:, at]), axis=1))
        result = right_mix(jnp.concatenate(turned, axis=0))
        return [
            (
                result[place * rows : (place + 1) * rows, :samples],
                result[place * rows : (place + 1) * rows, samples:],
            )
            for place in range(len(fields))
        ]

    wait_bytes(recv_a.at[pl.ds(0, tm_size - 1)], recv_sem.at[0])
    both = recv_a[...].astype(F32)
    value = stencil(both[:, :PACK], taps) * scale
    grad = both[:, PACK:]
    (vr, vi), (gr, gi) = forward([value.reshape(rows, samples), grad.reshape(rows, samples)])

    inverse_scale = 1.0 / (tm_size * samples)
    term_r = (vr * gr + vi * gi) * inverse_scale
    term_i = (vr * gi - vi * gr) * inverse_scale
    inner = right_mix(jnp.concatenate([term_r, -term_i], axis=1))
    inner_r, inner_i = twiddle(inner[:, :samples], inner[:, samples:])
    high_r, low_r = split(inner_r)
    high_i, low_i = split(inner_i)
    send_r[...] = to_blocks(
        dot(lh[:rows, :], high_r)
        + dot(ll[:rows, :], high_r)
        + dot(lh[:rows, :], low_r)
        - dot(lh[rows:, :], high_i)
        - dot(ll[rows:, :], high_i)
        - dot(lh[rows:, :], low_i)
    )

    @pl.when(adder != dp)
    def _():
        pl.semaphore_wait(plane_sem, 1)

    slot = dp * per + lax.rem(tm, per)

    def send_partial(block):
        pltpu.make_async_remote_copy(
            src_ref=send_r.at[block],
            dst_ref=recv_r.at[slot],
            send_sem=send_sem.at[2],
            recv_sem=recv_sem.at[2],
            device_id=(adder, block),
            device_id_type=MESH,
        ).start()

    @pl.loop(0, tm_size - 1)
    def _(step):
        send_partial(tm_peer(step))

    @pl.when(adder != dp)
    def _():
        send_partial(tm)

    @pl.when(adder == dp)
    def _():
        recv_r[slot] = send_r[tm]

    wait_bytes(recv_f.at[pl.ds(0, tm_size - 1)], recv_sem.at[1])
    ((fr, fi),) = forward([recv_f[...].reshape(rows, samples)])
    fr = fr * inverse_scale
    fi = fi * inverse_scale
    pr = vr * fr - vi * fi
    pi = vr * fi + vi * fr
    qr = gr * fr + gi * fi
    qi = gi * fr - gr * fi
    inner = right_mix(jnp.concatenate([pr - qi, -(pi + qr)], axis=1))
    inner = jnp.concatenate(twiddle(inner[:, :samples], inner[:, samples:]), axis=1)
    mixed = left_mix(inner)
    convolved = mixed[:rows, :samples] - mixed[rows:, samples:]
    correlated = -mixed[rows:, :samples] - mixed[:rows, samples:]

    send_l[...] = to_blocks(convolved) + gain * value
    exchange(send_l, recv_l, 3)
    middle = (to_blocks(correlated) + gain * grad) * scale
    send_w[...] = stencil(middle, taps[::-1])

    exchange(send_w, recv_w, 5)
    own_l = pltpu.make_async_copy(send_l.at[tm], recv_l.at[tm], local_sem.at[8])
    own_w = pltpu.make_async_copy(send_w.at[tm], recv_w.at[tm], local_sem.at[10])
    own_l.start()
    own_w.start()

    @pl.when(adder == dp)
    def _():
        wait_bytes(recv_r.at[pl.ds(0, tm_size - 1)], recv_sem.at[2])

    @pl.when(adder != dp)
    def _():
        wait_bytes(recv_r, recv_sem.at[2])

    send_g[...] = jnp.sum(recv_r[...].reshape(dp_size, per, PACK, samples), axis=0)
    summed = recv_g.at[pl.ds(dp * per, per)]

    @pl.loop(0, dp_size - 1)
    def _(step):
        pltpu.make_async_remote_copy(
            src_ref=send_g,
            dst_ref=summed,
            send_sem=send_sem.at[4],
            recv_sem=recv_sem.at[4],
            device_id=(dp_peer(step), tm),
            device_id_type=MESH,
        ).start()

    own_g = pltpu.make_async_copy(send_g, summed, local_sem.at[9])
    own_g.start()
    wait_bytes(send_a.at[pl.ds(0, tm_size - 1)], send_sem.at[0])
    wait_bytes(send_f.at[pl.ds(0, tm_size - 1)], send_sem.at[1])
    wait_bytes(send_l.at[pl.ds(0, tm_size - 1)], send_sem.at[3])
    wait_bytes(send_w.at[pl.ds(0, tm_size - 1)], send_sem.at[5])

    @pl.when(adder == dp)
    def _():
        wait_bytes(send_r.at[pl.ds(0, tm_size - 1)], send_sem.at[2])

    @pl.when(adder != dp)
    def _():
        wait_bytes(send_r, send_sem.at[2])

    wait_bytes(recv_r.at[pl.ds(0, tm_size - per)], send_sem.at[4])
    own_l.wait()
    own_w.wait()
    own_g.wait()
    wait_bytes(recv_l.at[pl.ds(0, tm_size - 1)], recv_sem.at[3])
    wait_bytes(recv_w.at[pl.ds(0, tm_size - 1)], recv_sem.at[5])
    wait_bytes(recv_g.at[pl.ds(0, tm_size - per)], recv_sem.at[4])


def turn_back(
    raw_layer, raw_gradw, raw_fgrad, layer_hbm, gradw_hbm, fgrad_hbm, raw, turned, load_sem, store_sem
):
    channels, samples = turned.shape[2], turned.shape[1]
    sources = [raw_layer, raw_gradw, raw_fgrad]
    targets = [layer_hbm, gradw_hbm, fgrad_hbm]
    loads = [
        pltpu.make_async_copy(sources[place], raw.at[place], load_sem.at[place])
        for place in range(3)
    ]
    stores = [
        pltpu.make_async_copy(turned.at[place], targets[place], store_sem.at[place])
        for place in range(3)
    ]
    for load in loads:
        load.start()
    for place in range(3):
        loads[place].wait()
        turned[place] = raw[place].reshape(channels, samples).T
        stores[place].start()
    for store in stores:
        store.wait()


def local(waveform, speaker_ids, speaker_table, stencil_taps, skip_gain, filters, cotangent):
    tm_size, dp_size = lax.axis_size("tm"), lax.axis_size("dp")
    samples, channels = filters.shape
    per = tm_size // dp_size
    rows = tm_size * PACK
    table = make_table(tm_size, samples)
    anywhere = pl.BlockSpec(memory_space=pl.ANY)
    block = jax.ShapeDtypeStruct((samples, channels), F32)
    pieces = jax.ShapeDtypeStruct((tm_size, PACK, samples), F32)
    received = pl.pallas_call(
        functools.partial(kernel, tm_size, dp_size),
        out_shape=[pieces] * 3,
        in_specs=[anywhere] * 8,
        out_specs=[anywhere] * 3,
        scratch_shapes=[
            pltpu.SMEM((1,), jnp.int32),
            pltpu.VMEM((samples, channels), BF16),
            pltpu.VMEM((samples, channels), BF16),
            pltpu.VMEM((samples, channels), F32),
            pltpu.VMEM(stencil_taps.shape, F32),
            pltpu.VMEM((1, channels), F32),
            pltpu.VMEM((speaker_table.shape[0] // ROWS16, ROWS16, channels), BF16),
            pltpu.VMEM(table.shape, F32),
            pltpu.VMEM((2 * rows, rows), BF16),
            pltpu.VMEM((2 * rows, rows), BF16),
            pltpu.VMEM((2 * samples, 2 * samples), BF16),
            pltpu.VMEM((2 * samples, 2 * samples), BF16),
            pltpu.VMEM((tm_size, 2 * PACK, samples), BF16),
            pltpu.VMEM((tm_size, 2 * PACK, samples), BF16),
            pltpu.VMEM((tm_size, PACK, samples), F32),
            pltpu.VMEM((tm_size, PACK, samples), F32),
            pltpu.VMEM((tm_size, PACK, samples), F32),
            pltpu.VMEM((tm_size, PACK, samples), F32),
            pltpu.VMEM((tm_size, PACK, samples), F32),
            pltpu.VMEM((tm_size, PACK, samples), F32),
            pltpu.VMEM((per, PACK, samples), F32),
            pltpu.SemaphoreType.DMA((11,)),
            pltpu.SemaphoreType.DMA((6,)),
            pltpu.SemaphoreType.DMA((6,)),
            pltpu.SemaphoreType.REGULAR,
        ],
        compiler_params=pltpu.CompilerParams(
            collective_id=0, has_side_effects=True, vmem_limit_bytes=62 * 1024 * 1024
        ),
    )(
        speaker_ids,
        waveform[0],
        cotangent[0],
        filters,
        stencil_taps,
        skip_gain[None],
        speaker_table.reshape(-1, ROWS16, channels),
        jnp.asarray(table),
    )
    layer_out, grad_waveform, filter_grad = pl.pallas_call(
        turn_back,
        out_shape=[block, block, block],
        in_specs=[anywhere] * 3,
        out_specs=[anywhere] * 3,
        scratch_shapes=[
            pltpu.VMEM((3, tm_size, PACK, samples), F32),
            pltpu.VMEM((3, samples, channels), F32),
            pltpu.SemaphoreType.DMA((3,)),
            pltpu.SemaphoreType.DMA((3,)),
        ],
        compiler_params=pltpu.CompilerParams(vmem_limit_bytes=62 * 1024 * 1024),
    )(*received)
    return layer_out[None], grad_waveform[None], filter_grad


def solution(mesh):
    return jax.shard_map(
        local,
        mesh=mesh,
        in_specs=(P("dp", "tm", None), P("dp"), P(), P(), P(), P("tm", None), P("dp", "tm", None)),
        out_specs=(P("dp", "tm", None), P("dp", "tm", None), P("tm", None)),
        check_vma=False,
    )
```

```python
import functools
import math

import jax
import jax.numpy as jnp
import numpy as np
from jax import lax
from jax.experimental import pallas as pl
from jax.experimental.pallas import tpu as pltpu
from jax.sharding import PartitionSpec as P

MESH = pl.DeviceIdType.MESH
F32 = jnp.float32
BF16 = jnp.bfloat16
PACK = 8
ROWS16 = 16


def make_table(blocks, samples):
    total = blocks * samples
    spread = np.eye(PACK)
    block = np.arange(blocks)
    low = np.arange(blocks // 2 + 1)
    angle = 2.0 * math.pi / blocks * (np.outer(low, block) % blocks)
    forward = np.concatenate([np.cos(angle), -np.sin(angle)[1:-1]])
    weight = np.where((low == 0) | (low == blocks // 2), 1.0, 2.0)[:, None] / total
    backward = np.concatenate([weight * np.cos(angle), (weight * np.sin(angle))[1:-1]]).T
    inner = np.arange(samples)
    angle = 2.0 * math.pi / samples * (np.outer(inner, inner) % samples)
    right = np.block([[np.cos(angle), -np.sin(angle)], [np.sin(angle), np.cos(angle)]])
    turn = np.repeat(2.0 * math.pi / total * np.outer(low, inner), PACK, axis=0)
    turn = np.concatenate([np.cos(turn), np.sin(turn)], axis=1)
    parts = [np.kron(forward, spread), np.kron(backward, spread), right, turn]
    wide = max(part.shape[1] for part in parts)
    parts = [np.pad(part, ((0, 0), (0, wide - part.shape[1]))) for part in parts]
    return np.concatenate(parts).astype(np.float32)


def split(array):
    high = array.astype(BF16)
    return high, (array - high.astype(F32)).astype(BF16)


def dot(a, b):
    return jnp.dot(a, b, preferred_element_type=F32)


def quantize(field):
    peak = jnp.max(jnp.abs(field), axis=2, keepdims=True)
    power = jnp.floor(4.0 * jnp.log2(32000.0 / jnp.maximum(peak, 1e-30)))
    return jnp.round(field * jnp.exp2(0.25 * power)).astype(jnp.int32), power + 512.0


def step_size(power):
    return jnp.exp2(0.25 * (512.0 - power))


def diagonal(blocks, lanes):
    shape = (blocks, PACK, lanes)
    return lax.broadcasted_iota(jnp.int32, shape, 1) == lax.broadcasted_iota(jnp.int32, shape, 2)


def lay_out(power, lanes):
    spread = jnp.where(diagonal(power.shape[0], lanes), power, 0.0)
    return jnp.sum(spread, axis=1, keepdims=True).astype(jnp.int32)


def stand_up(row):
    spread = jnp.where(diagonal(row.shape[0], row.shape[2]), row.astype(F32), 0.0)
    return jnp.sum(spread, axis=2, keepdims=True)


def pair(high, low):
    return (high << 16) | (low & 0xFFFF)


def first_of(word):
    return (word >> 16).astype(F32)


def second_of(word):
    return ((word << 16) >> 16).astype(F32)


def encode_one(field, target):
    steps, power = quantize(field)
    half = PACK // 2
    target[:, :half] = pair(steps, pltpu.roll(steps, half, 1))[:, :half]
    target[:, half:] = lay_out(power, field.shape[2])


def decode_one(source):
    half = PACK // 2
    words = source[:, :half]
    power = stand_up(source[:, half:])
    return jnp.concatenate([first_of(words), second_of(words)], axis=1) * step_size(power)


def encode_two(first, second, target):
    first_steps, first_power = quantize(first)
    second_steps, second_power = quantize(second)
    target[:, :PACK] = pair(first_steps, second_steps)
    target[:, PACK:] = lay_out(first_power + 1024.0 * second_power, first.shape[2])


def decode_two(source):
    words = source[:, :PACK]
    powers = stand_up(source[:, PACK:]).astype(jnp.int32)
    first_power = (powers & 1023).astype(F32)
    second_power = (powers >> 10).astype(F32)
    return first_of(words) * step_size(first_power), second_of(words) * step_size(second_power)


def far_first(step, size):
    shift = lax.div(step + 1, 2)
    return lax.rem(size + size // 2 + jnp.where(lax.rem(step, 2) == 1, -shift, shift), size)


def stencil(field, taps):
    lanes = field.shape[2]
    lane = lax.broadcasted_iota(jnp.int32, field.shape, 2)
    edge = jnp.zeros((1,) + field.shape[1:], F32)
    turned = pltpu.roll(field, 1, 2)
    before = jnp.where(lane == 0, jnp.concatenate([edge, turned[:-1]], axis=0), turned)
    turned = pltpu.roll(field, lanes - 1, 2)
    after = jnp.where(lane == lanes - 1, jnp.concatenate([turned[1:], edge], axis=0), turned)
    return taps[0] * before + taps[1] * field + taps[2] * after


def kernel(
    tm_size,
    dp_size,
    ids_hbm,
    wave_hbm,
    cot_hbm,
    filt_hbm,
    taps_hbm,
    gain_hbm,
    speakers_hbm,
    table_hbm,
    recv_c,
    recv_g,
    ids,
    wave_ref,
    cot_ref,
    filt_ref,
    taps_ref,
    gain_ref,
    speakers,
    table,
    lh,
    ll,
    bh,
    bl,
    rh,
    rl,
    send_a,
    recv_a,
    send_f,
    recv_f,
    send_c,
    send_r,
    recv_r,
    send_g,
    local_sem,
    send_sem,
    recv_sem,
    plane_sem,
):
    dp = lax.axis_index("dp")
    tm = lax.axis_index("tm")
    per = tm_size // dp_size
    place = lax.div(tm, dp_size)
    column_at = lax.rem(tm, dp_size)
    samples = wave_ref.shape[0]
    channels = wave_ref.shape[1]
    rows = tm_size * PACK

    barrier = pltpu.get_barrier_semaphore()

    def tm_peer(step):
        far = far_first(lax.div(step, per), dp_size)
        across = far_first(lax.rem(step, per), per)
        return lax.rem(place + across, per) * dp_size + lax.rem(column_at + far, dp_size)

    def dp_peer(step):
        return lax.rem(dp + far_first(step, dp_size), dp_size)

    @pl.loop(0, tm_size - 1)
    def _(step):
        pl.semaphore_signal(barrier, inc=1, device_id=(dp, tm_peer(step)), device_id_type=MESH)

    @pl.loop(0, dp_size - 1)
    def _(step):
        pl.semaphore_signal(barrier, inc=1, device_id=(dp_peer(step), tm), device_id_type=MESH)

    pairs = [
        (wave_hbm, wave_ref),
        (cot_hbm, cot_ref),
        (filt_hbm, filt_ref),
        (table_hbm, table),
        (taps_hbm, taps_ref),
        (gain_hbm, gain_ref),
        (ids_hbm, ids),
        (speakers_hbm, speakers),
    ]
    loads = [
        pltpu.make_async_copy(source, target, local_sem.at[slot])
        for slot, (source, target) in enumerate(pairs)
    ]

    def wait_bytes(like, sem):
        pltpu.make_async_copy(like, like, sem).wait()

    def exchange(source, target, which):
        @pl.loop(0, tm_size - 1)
        def _(step):
            peer = tm_peer(step)
            pltpu.make_async_remote_copy(
                src_ref=source.at[peer],
                dst_ref=target.at[tm],
                send_sem=send_sem.at[which],
                recv_sem=recv_sem.at[which],
                device_id=(dp, peer),
                device_id_type=MESH,
            ).start()

    def to_blocks(field):
        return field.reshape(tm_size, PACK, samples)

    for load in loads[:3]:
        load.start()
    loads[0].wait()
    wave_t = to_blocks(wave_ref[...].astype(F32).T)
    loads[1].wait()
    cot_t = to_blocks(cot_ref[...].astype(F32).T)
    send_a[...] = jnp.concatenate([wave_t, cot_t], axis=1).astype(BF16)
    pl.semaphore_wait(barrier, tm_size - 1 + dp_size - 1)
    exchange(send_a, recv_a, 0)
    recv_a[tm] = send_a[tm]

    adder = lax.div(tm, per)

    @pl.when(adder == dp)
    def _():
        @pl.loop(0, dp_size - 1)
        def _(step):
            pl.semaphore_signal(plane_sem, inc=1, device_id=(dp_peer(step), tm), device_id_type=MESH)

    loads[2].wait()
    encode_one(to_blocks(filt_ref[...].T), send_f)
    exchange(send_f, recv_f, 1)
    recv_f[tm] = send_f[tm]

    for load in loads[3:]:
        load.start()
    for load in loads[3:]:
        load.wait()
    lh[...], ll[...] = split(table[:rows, :rows])
    bh[...], bl[...] = split(table[rows : 2 * rows, :rows])
    rh[...], rl[...] = split(table[2 * rows : 2 * rows + 2 * samples, : 2 * samples])
    tc = table[2 * rows + 2 * samples :, :samples]
    ts = table[2 * rows + 2 * samples :, samples : 2 * samples]
    lane = lax.broadcasted_iota(jnp.int32, (PACK, channels), 1)
    row = lax.broadcasted_iota(jnp.int32, (PACK, channels), 0)
    mine = lane == tm * PACK + row

    def column(vector):
        return jnp.sum(jnp.where(mine, vector, 0.0), axis=1, keepdims=True)

    speaker = ids[0]
    group = speakers[lax.div(speaker, ROWS16)]
    picked = lax.broadcasted_iota(jnp.int32, (ROWS16, channels), 0) == lax.rem(speaker, ROWS16)
    speaker_row = jnp.sum(jnp.where(picked, group.astype(F32), 0.0), axis=0, keepdims=True)
    scale = column(speaker_row)
    taps = [column(taps_ref[place : place + 1, :]) for place in range(3)]
    gain = column(gain_ref[...])

    def right_mix(field):
        high, low = split(field)
        return dot(high, rh[...]) + (dot(high, rl[...]) + dot(low, rh[...]))

    def twiddle(real, imag):
        return real * tc + imag * ts, imag * tc - real * ts

    half_rows = (tm_size // 2 + 1) * PACK

    def forward(mixed):
        count = mixed.shape[1] // samples
        blank = jnp.zeros((PACK, samples), F32)
        turned = []
        for field in range(count):
            part = mixed[:, field * samples : (field + 1) * samples]
            imag = jnp.concatenate([blank, part[half_rows:], blank], axis=0)
            turned.append(jnp.concatenate(twiddle(part[:half_rows], imag), axis=1))
        result = right_mix(jnp.concatenate(turned, axis=0))
        parts = [result[field * half_rows : (field + 1) * half_rows] for field in range(count)]
        return [(part[:, :samples], part[:, samples:]) for part in parts]

    def backward(spectra):
        packed = [jnp.concatenate([real, -imag], axis=1) for real, imag in spectra]
        inner = right_mix(jnp.concatenate(packed, axis=0))
        turned = []
        for field in range(len(spectra)):
            part = inner[field * half_rows : (field + 1) * half_rows]
            real, imag = twiddle(part[:, :samples], part[:, samples:])
            turned.append(jnp.concatenate([real, imag[PACK:-PACK]], axis=0))
        high, low = split(jnp.concatenate(turned, axis=1))
        return dot(bh[...], high) + (dot(bl[...], high) + dot(bh[...], low))

    wait_bytes(recv_a.at[pl.ds(0, tm_size - 1)], recv_sem.at[0])
    both = recv_a[...].astype(F32)
    value = stencil(both[:, :PACK], taps) * scale
    grad = both[:, PACK:]
    value_high, value_low = split(value.reshape(rows, samples))
    high = jnp.concatenate([value_high, grad.reshape(rows, samples).astype(BF16)], axis=1)
    mixed = dot(lh[...], high) + dot(ll[...], high)
    mixed_value = mixed[:, :samples] + dot(lh[...], value_low)
    mixed = jnp.concatenate([mixed_value, mixed[:, samples:]], axis=1)
    (vr, vi), (gr, gi) = forward(mixed)
    encode_one(to_blocks(backward([(vr * gr + vi * gi, vr * gi - vi * gr)])), send_r)

    @pl.when(adder != dp)
    def _():
        pl.semaphore_wait(plane_sem, 1)

    slot = dp * per + lax.rem(tm, per)

    def send_partial(block):
        pltpu.make_async_remote_copy(
            src_ref=send_r.at[block],
            dst_ref=recv_r.at[slot],
            send_sem=send_sem.at[2],
            recv_sem=recv_sem.at[2],
            device_id=(adder, block),
            device_id_type=MESH,
        ).start()

    @pl.loop(0, tm_size - 1)
    def _(step):
        send_partial(tm_peer(step))

    @pl.when(adder != dp)
    def _():
        send_partial(tm)

    @pl.when(adder == dp)
    def _():
        recv_r[slot] = send_r[tm]

    wait_bytes(recv_f.at[pl.ds(0, tm_size - 1)], recv_sem.at[1])
    high, low = split(decode_one(recv_f).reshape(rows, samples))
    ((fr, fi),) = forward(dot(lh[...], high) + (dot(ll[...], high) + dot(lh[...], low)))
    results = backward(
        [
            (vr * fr - vi * fi, vr * fi + vi * fr),
            (gr * fr + gi * fi, gi * fr - gr * fi),
        ]
    )
    convolved, correlated = results[:, :samples], results[:, samples:]
    layer = to_blocks(convolved) + gain * value
    middle = (to_blocks(correlated) + gain * grad) * scale
    encode_two(layer, stencil(middle, taps[::-1]), send_c)
    exchange(send_c, recv_c, 3)
    own_c = pltpu.make_async_copy(send_c.at[tm], recv_c.at[tm], local_sem.at[8])
    own_c.start()

    @pl.when(adder == dp)
    def _():
        wait_bytes(recv_r.at[pl.ds(0, tm_size - 1)], recv_sem.at[2])

    @pl.when(adder != dp)
    def _():
        wait_bytes(recv_r, recv_sem.at[2])

    send_g[...] = jnp.sum(decode_one(recv_r).reshape(dp_size, per, PACK, samples), axis=0)
    summed = recv_g.at[pl.ds(dp * per, per)]

    @pl.loop(0, dp_size - 1)
    def _(step):
        pltpu.make_async_remote_copy(
            src_ref=send_g,
            dst_ref=summed,
            send_sem=send_sem.at[4],
            recv_sem=recv_sem.at[4],
            device_id=(dp_peer(step), tm),
            device_id_type=MESH,
        ).start()

    own_g = pltpu.make_async_copy(send_g, summed, local_sem.at[9])
    own_g.start()
    wait_bytes(send_a.at[pl.ds(0, tm_size - 1)], send_sem.at[0])
    wait_bytes(send_f.at[pl.ds(0, tm_size - 1)], send_sem.at[1])
    wait_bytes(send_c.at[pl.ds(0, tm_size - 1)], send_sem.at[3])

    @pl.when(adder == dp)
    def _():
        wait_bytes(send_r.at[pl.ds(0, tm_size - 1)], send_sem.at[2])

    @pl.when(adder != dp)
    def _():
        wait_bytes(send_r, send_sem.at[2])

    wait_bytes(recv_g.at[pl.ds(0, tm_size - per)], send_sem.at[4])
    own_c.wait()
    own_g.wait()
    wait_bytes(recv_c.at[pl.ds(0, tm_size - 1)], recv_sem.at[3])
    wait_bytes(recv_g.at[pl.ds(0, tm_size - per)], recv_sem.at[4])


def turn_back(
    coded_hbm, third_hbm, layer_hbm, gradw_hbm, fgrad_hbm, coded, third, turned, load_sem, store_sem
):
    channels, samples = turned.shape[2], turned.shape[1]
    loads = [
        pltpu.make_async_copy(coded_hbm, coded, load_sem.at[0]),
        pltpu.make_async_copy(third_hbm, third, load_sem.at[1]),
    ]
    targets = [layer_hbm, gradw_hbm, fgrad_hbm]
    stores = [
        pltpu.make_async_copy(turned.at[place], targets[place], store_sem.at[place])
        for place in range(3)
    ]

    def turn(place, field):
        turned[place] = field.reshape(channels, samples).T
        stores[place].start()

    for load in loads:
        load.start()
    loads[0].wait()
    layer, gradw = decode_two(coded)
    turn(0, layer)
    turn(1, gradw)
    loads[1].wait()
    turn(2, third[...])
    for store in stores:
        store.wait()


def local(waveform, speaker_ids, speaker_table, stencil_taps, skip_gain, filters, cotangent):
    tm_size, dp_size = lax.axis_size("tm"), lax.axis_size("dp")
    samples, channels = filters.shape
    per = tm_size // dp_size
    rows = tm_size * PACK
    table = make_table(tm_size, samples)
    anywhere = pl.BlockSpec(memory_space=pl.ANY)
    block = jax.ShapeDtypeStruct((samples, channels), F32)
    coded = jax.ShapeDtypeStruct((tm_size, PACK + 1, samples), jnp.int32)
    pieces = jax.ShapeDtypeStruct((tm_size, PACK, samples), F32)
    received = pl.pallas_call(
        functools.partial(kernel, tm_size, dp_size),
        out_shape=[coded, pieces],
        in_specs=[anywhere] * 8,
        out_specs=[anywhere] * 2,
        scratch_shapes=[
            pltpu.SMEM((1,), jnp.int32),
            pltpu.VMEM((samples, channels), BF16),
            pltpu.VMEM((samples, channels), BF16),
            pltpu.VMEM((samples, channels), F32),
            pltpu.VMEM(stencil_taps.shape, F32),
            pltpu.VMEM((1, channels), F32),
            pltpu.VMEM((speaker_table.shape[0] // ROWS16, ROWS16, channels), BF16),
            pltpu.VMEM(table.shape, F32),
            *[pltpu.VMEM((rows, rows), BF16)] * 4,
            pltpu.VMEM((2 * samples, 2 * samples), BF16),
            pltpu.VMEM((2 * samples, 2 * samples), BF16),
            pltpu.VMEM((tm_size, 2 * PACK, samples), BF16),
            pltpu.VMEM((tm_size, 2 * PACK, samples), BF16),
            pltpu.VMEM((tm_size, PACK // 2 + 1, samples), jnp.int32),
            pltpu.VMEM((tm_size, PACK // 2 + 1, samples), jnp.int32),
            pltpu.VMEM((tm_size, PACK + 1, samples), jnp.int32),
            pltpu.VMEM((tm_size, PACK // 2 + 1, samples), jnp.int32),
            pltpu.VMEM((tm_size, PACK // 2 + 1, samples), jnp.int32),
            pltpu.VMEM((per, PACK, samples), F32),
            pltpu.SemaphoreType.DMA((11,)),
            pltpu.SemaphoreType.DMA((6,)),
            pltpu.SemaphoreType.DMA((6,)),
            pltpu.SemaphoreType.REGULAR,
        ],
        compiler_params=pltpu.CompilerParams(
            collective_id=0, has_side_effects=True, vmem_limit_bytes=62 * 1024 * 1024
        ),
    )(
        speaker_ids,
        waveform[0],
        cotangent[0],
        filters,
        stencil_taps,
        skip_gain[None],
        speaker_table.reshape(-1, ROWS16, channels),
        jnp.asarray(table),
    )
    layer_out, grad_waveform, filter_grad = pl.pallas_call(
        turn_back,
        out_shape=[block, block, block],
        in_specs=[anywhere] * 2,
        out_specs=[anywhere] * 3,
        scratch_shapes=[
            pltpu.VMEM(coded.shape, jnp.int32),
            pltpu.VMEM(pieces.shape, F32),
            pltpu.VMEM((3, samples, channels), F32),
            pltpu.SemaphoreType.DMA((2,)),
            pltpu.SemaphoreType.DMA((3,)),
        ],
        compiler_params=pltpu.CompilerParams(vmem_limit_bytes=62 * 1024 * 1024),
    )(*received)
    return layer_out[None], grad_waveform[None], filter_grad


def solution(mesh):
    return jax.shard_map(
        local,
        mesh=mesh,
        in_specs=(P("dp", "tm", None), P("dp"), P(), P(), P(), P("tm", None), P("dp", "tm", None)),
        out_specs=(P("dp", "tm", None), P("dp", "tm", None), P("tm", None)),
        check_vma=False,
    )
```

```python
import functools
import math

import jax
import jax.numpy as jnp
import numpy as np
from jax import lax
from jax.experimental import pallas as pl
from jax.experimental.pallas import tpu as pltpu
from jax.sharding import PartitionSpec as P

MESH = pl.DeviceIdType.MESH
F32 = jnp.float32
BF16 = jnp.bfloat16
PACK = 8
ROWS16 = 16


def make_table(blocks, samples):
    total = blocks * samples
    spread = np.eye(PACK)
    block = np.arange(blocks)
    low = np.arange(blocks // 2 + 1)
    angle = 2.0 * math.pi / blocks * (np.outer(low, block) % blocks)
    forward = np.concatenate([np.cos(angle), -np.sin(angle)[1:-1]])
    weight = np.where((low == 0) | (low == blocks // 2), 1.0, 2.0)[:, None] / total
    backward = np.concatenate([weight * np.cos(angle), (weight * np.sin(angle))[1:-1]]).T
    inner = np.arange(samples)
    angle = 2.0 * math.pi / samples * (np.outer(inner, inner) % samples)
    right = np.block([[np.cos(angle), -np.sin(angle)], [np.sin(angle), np.cos(angle)]])
    turn = np.repeat(2.0 * math.pi / total * np.outer(low, inner), PACK, axis=0)
    turn = np.concatenate([np.cos(turn), np.sin(turn)], axis=1)
    parts = [np.kron(forward, spread), np.kron(backward, spread), right, turn]
    wide = max(part.shape[1] for part in parts)
    parts = [np.pad(part, ((0, 0), (0, wide - part.shape[1]))) for part in parts]
    return np.concatenate(parts).astype(np.float32)


def split(array):
    high = array.astype(BF16)
    return high, (array - high.astype(F32)).astype(BF16)


def dot(a, b):
    return jnp.dot(a, b, preferred_element_type=F32)


def quantize(field):
    peak = jnp.max(jnp.abs(field), axis=2, keepdims=True)
    power = jnp.floor(4.0 * jnp.log2(32000.0 / jnp.maximum(peak, 1e-30)))
    return jnp.round(field * jnp.exp2(0.25 * power)).astype(jnp.int32), power + 512.0


def step_size(power):
    return jnp.exp2(0.25 * (512.0 - power))


def diagonal(blocks, lanes):
    shape = (blocks, PACK, lanes)
    return lax.broadcasted_iota(jnp.int32, shape, 1) == lax.broadcasted_iota(jnp.int32, shape, 2)


def lay_out(power, lanes):
    spread = jnp.where(diagonal(power.shape[0], lanes), power, 0.0)
    return jnp.sum(spread, axis=1, keepdims=True).astype(jnp.int32)


def stand_up(row):
    spread = jnp.where(diagonal(row.shape[0], row.shape[2]), row.astype(F32), 0.0)
    return jnp.sum(spread, axis=2, keepdims=True)


def pair(high, low):
    return (high << 16) | (low & 0xFFFF)


def first_of(word):
    return (word >> 16).astype(F32)


def second_of(word):
    return ((word << 16) >> 16).astype(F32)


def encode_one(field, target):
    steps, power = quantize(field)
    half = PACK // 2
    target[:, :half] = pair(steps, pltpu.roll(steps, half, 1))[:, :half]
    target[:, half:] = lay_out(power, field.shape[2])


def decode_one(source):
    half = PACK // 2
    words = source[:, :half]
    power = stand_up(source[:, half:])
    return jnp.concatenate([first_of(words), second_of(words)], axis=1) * step_size(power)


def encode_two(first, second, target):
    first_steps, first_power = quantize(first)
    second_steps, second_power = quantize(second)
    target[:, :PACK] = pair(first_steps, second_steps)
    target[:, PACK:] = lay_out(first_power + 1024.0 * second_power, first.shape[2])


def decode_two(source):
    words = source[:, :PACK]
    powers = stand_up(source[:, PACK:]).astype(jnp.int32)
    first_power = (powers & 1023).astype(F32)
    second_power = (powers >> 10).astype(F32)
    return first_of(words) * step_size(first_power), second_of(words) * step_size(second_power)


def far_first(step, size):
    shift = lax.div(step + 1, 2)
    return lax.rem(size + size // 2 + jnp.where(lax.rem(step, 2) == 1, -shift, shift), size)


def stencil(field, taps):
    lanes = field.shape[2]
    lane = lax.broadcasted_iota(jnp.int32, field.shape, 2)
    edge = jnp.zeros((1,) + field.shape[1:], F32)
    turned = pltpu.roll(field, 1, 2)
    before = jnp.where(lane == 0, jnp.concatenate([edge, turned[:-1]], axis=0), turned)
    turned = pltpu.roll(field, lanes - 1, 2)
    after = jnp.where(lane == lanes - 1, jnp.concatenate([turned[1:], edge], axis=0), turned)
    return taps[0] * before + taps[1] * field + taps[2] * after


def kernel(
    tm_size,
    dp_size,
    ids_hbm,
    wave_hbm,
    cot_hbm,
    filt_hbm,
    taps_hbm,
    gain_hbm,
    speakers_hbm,
    table_hbm,
    layer_hbm,
    gradw_hbm,
    recv_g,
    ids,
    wave_ref,
    cot_ref,
    filt_ref,
    taps_ref,
    gain_ref,
    speakers,
    table,
    lh,
    ll,
    bh,
    bl,
    rh,
    rl,
    send_a,
    recv_a,
    send_f,
    recv_f,
    send_c,
    recv_c,
    turned,
    send_r,
    recv_r,
    send_g,
    local_sem,
    send_sem,
    recv_sem,
    plane_sem,
):
    dp = lax.axis_index("dp")
    tm = lax.axis_index("tm")
    per = tm_size // dp_size
    place = lax.div(tm, dp_size)
    column_at = lax.rem(tm, dp_size)
    samples = wave_ref.shape[0]
    channels = wave_ref.shape[1]
    rows = tm_size * PACK

    barrier = pltpu.get_barrier_semaphore()

    def tm_peer(step):
        far = far_first(lax.div(step, per), dp_size)
        across = far_first(lax.rem(step, per), per)
        return lax.rem(place + across, per) * dp_size + lax.rem(column_at + far, dp_size)

    def dp_peer(step):
        return lax.rem(dp + far_first(step, dp_size), dp_size)

    @pl.loop(0, tm_size - 1)
    def _(step):
        pl.semaphore_signal(barrier, inc=1, device_id=(dp, tm_peer(step)), device_id_type=MESH)

    @pl.loop(0, dp_size - 1)
    def _(step):
        pl.semaphore_signal(barrier, inc=1, device_id=(dp_peer(step), tm), device_id_type=MESH)

    pairs = [
        (wave_hbm, wave_ref),
        (cot_hbm, cot_ref),
        (filt_hbm, filt_ref),
        (table_hbm, table),
        (taps_hbm, taps_ref),
        (gain_hbm, gain_ref),
        (ids_hbm, ids),
        (speakers_hbm, speakers),
    ]
    loads = [
        pltpu.make_async_copy(source, target, local_sem.at[slot])
        for slot, (source, target) in enumerate(pairs)
    ]

    def wait_bytes(like, sem):
        pltpu.make_async_copy(like, like, sem).wait()

    def exchange(source, target, which):
        @pl.loop(0, tm_size - 1)
        def _(step):
            peer = tm_peer(step)
            pltpu.make_async_remote_copy(
                src_ref=source.at[peer],
                dst_ref=target.at[tm],
                send_sem=send_sem.at[which],
                recv_sem=recv_sem.at[which],
                device_id=(dp, peer),
                device_id_type=MESH,
            ).start()

    def to_blocks(field):
        return field.reshape(tm_size, PACK, samples)

    for load in loads[:3]:
        load.start()
    loads[0].wait()
    wave_t = to_blocks(wave_ref[...].astype(F32).T)
    loads[1].wait()
    cot_t = to_blocks(cot_ref[...].astype(F32).T)
    send_a[...] = jnp.concatenate([wave_t, cot_t], axis=1).astype(BF16)
    pl.semaphore_wait(barrier, tm_size - 1 + dp_size - 1)
    exchange(send_a, recv_a, 0)
    recv_a[tm] = send_a[tm]

    adder = lax.div(tm, per)

    @pl.when(adder == dp)
    def _():
        @pl.loop(0, dp_size - 1)
        def _(step):
            pl.semaphore_signal(plane_sem, inc=1, device_id=(dp_peer(step), tm), device_id_type=MESH)

    loads[2].wait()
    encode_one(to_blocks(filt_ref[...].T), send_f)
    exchange(send_f, recv_f, 1)
    recv_f[tm] = send_f[tm]

    for load in loads[3:]:
        load.start()
    for load in loads[3:]:
        load.wait()
    lh[...], ll[...] = split(table[:rows, :rows])
    bh[...], bl[...] = split(table[rows : 2 * rows, :rows])
    rh[...], rl[...] = split(table[2 * rows : 2 * rows + 2 * samples, : 2 * samples])
    tc = table[2 * rows + 2 * samples :, :samples]
    ts = table[2 * rows + 2 * samples :, samples : 2 * samples]
    lane = lax.broadcasted_iota(jnp.int32, (PACK, channels), 1)
    row = lax.broadcasted_iota(jnp.int32, (PACK, channels), 0)
    mine = lane == tm * PACK + row

    def column(vector):
        return jnp.sum(jnp.where(mine, vector, 0.0), axis=1, keepdims=True)

    speaker = ids[0]
    group = speakers[lax.div(speaker, ROWS16)]
    picked = lax.broadcasted_iota(jnp.int32, (ROWS16, channels), 0) == lax.rem(speaker, ROWS16)
    speaker_row = jnp.sum(jnp.where(picked, group.astype(F32), 0.0), axis=0, keepdims=True)
    scale = column(speaker_row)
    taps = [column(taps_ref[place : place + 1, :]) for place in range(3)]
    gain = column(gain_ref[...])

    def right_mix(field):
        high, low = split(field)
        return dot(high, rh[...]) + (dot(high, rl[...]) + dot(low, rh[...]))

    def twiddle(real, imag):
        return real * tc + imag * ts, imag * tc - real * ts

    half_rows = (tm_size // 2 + 1) * PACK

    def forward(mixed):
        count = mixed.shape[1] // samples
        blank = jnp.zeros((PACK, samples), F32)
        turned = []
        for field in range(count):
            part = mixed[:, field * samples : (field + 1) * samples]
            imag = jnp.concatenate([blank, part[half_rows:], blank], axis=0)
            turned.append(jnp.concatenate(twiddle(part[:half_rows], imag), axis=1))
        result = right_mix(jnp.concatenate(turned, axis=0))
        parts = [result[field * half_rows : (field + 1) * half_rows] for field in range(count)]
        return [(part[:, :samples], part[:, samples:]) for part in parts]

    def backward(spectra):
        packed = [jnp.concatenate([real, -imag], axis=1) for real, imag in spectra]
        inner = right_mix(jnp.concatenate(packed, axis=0))
        turned = []
        for field in range(len(spectra)):
            part = inner[field * half_rows : (field + 1) * half_rows]
            real, imag = twiddle(part[:, :samples], part[:, samples:])
            turned.append(jnp.concatenate([real, imag[PACK:-PACK]], axis=0))
        high, low = split(jnp.concatenate(turned, axis=1))
        return dot(bh[...], high) + (dot(bl[...], high) + dot(bh[...], low))

    wait_bytes(recv_a.at[pl.ds(0, tm_size - 1)], recv_sem.at[0])
    both = recv_a[...].astype(F32)
    value = stencil(both[:, :PACK], taps) * scale
    grad = both[:, PACK:]
    value_high, value_low = split(value.reshape(rows, samples))
    high = jnp.concatenate([value_high, grad.reshape(rows, samples).astype(BF16)], axis=1)
    mixed = dot(lh[...], high) + dot(ll[...], high)
    mixed_value = mixed[:, :samples] + dot(lh[...], value_low)
    mixed = jnp.concatenate([mixed_value, mixed[:, samples:]], axis=1)
    (vr, vi), (gr, gi) = forward(mixed)
    send_r[...] = to_blocks(backward([(vr * gr + vi * gi, vr * gi - vi * gr)]))

    @pl.when(adder != dp)
    def _():
        pl.semaphore_wait(plane_sem, 1)

    slot = dp * per + lax.rem(tm, per)

    def send_partial(block):
        pltpu.make_async_remote_copy(
            src_ref=send_r.at[block],
            dst_ref=recv_r.at[slot],
            send_sem=send_sem.at[2],
            recv_sem=recv_sem.at[2],
            device_id=(adder, block),
            device_id_type=MESH,
        ).start()

    @pl.loop(0, tm_size)
    def _(step):
        block = lax.rem(place + far_first(lax.rem(step, per), per), per) * dp_size + lax.div(step, per)

        @pl.when(jnp.logical_not((block == tm) & (adder == dp)))
        def _():
            send_partial(block)

    @pl.when(adder == dp)
    def _():
        recv_r[slot] = send_r[tm]

    wait_bytes(recv_f.at[pl.ds(0, tm_size - 1)], recv_sem.at[1])
    high, low = split(decode_one(recv_f).reshape(rows, samples))
    ((fr, fi),) = forward(dot(lh[...], high) + (dot(ll[...], high) + dot(lh[...], low)))
    results = backward(
        [
            (vr * fr - vi * fi, vr * fi + vi * fr),
            (gr * fr + gi * fi, gi * fr - gr * fi),
        ]
    )
    convolved, correlated = results[:, :samples], results[:, samples:]
    layer = to_blocks(convolved) + gain * value
    middle = (to_blocks(correlated) + gain * grad) * scale
    encode_two(layer, stencil(middle, taps[::-1]), send_c)
    @pl.loop(0, tm_size)
    def _(step):
        peer = lax.rem(place + far_first(lax.rem(step, per), per), per) * dp_size + lax.div(step, per)

        @pl.when(peer != tm)
        def _():
            pltpu.make_async_remote_copy(
                src_ref=send_c.at[peer],
                dst_ref=recv_c.at[tm],
                send_sem=send_sem.at[3],
                recv_sem=recv_sem.at[3],
                device_id=(dp, peer),
                device_id_type=MESH,
            ).start()

    recv_c[tm] = send_c[tm]

    @pl.when(adder == dp)
    def _():
        wait_bytes(recv_r.at[pl.ds(0, tm_size - 1)], recv_sem.at[2])

    @pl.when(adder != dp)
    def _():
        wait_bytes(recv_r, recv_sem.at[2])

    send_g[...] = jnp.sum(recv_r[...].reshape(dp_size, per, PACK, samples), axis=0)
    summed = recv_g.at[pl.ds(dp * per, per)]

    @pl.loop(0, dp_size - 1)
    def _(step):
        pltpu.make_async_remote_copy(
            src_ref=send_g,
            dst_ref=summed,
            send_sem=send_sem.at[4],
            recv_sem=recv_sem.at[4],
            device_id=(dp_peer(step), tm),
            device_id_type=MESH,
        ).start()

    own_g = pltpu.make_async_copy(send_g, summed, local_sem.at[9])
    own_g.start()
    wait_bytes(recv_c.at[pl.ds(0, tm_size - 1)], recv_sem.at[3])
    stores = []
    for place_out, (field, target) in enumerate(zip(decode_two(recv_c), (layer_hbm, gradw_hbm))):
        turned[place_out] = field.reshape(channels, samples).T
        stores.append(
            pltpu.make_async_copy(turned.at[place_out], target, local_sem.at[8 + 2 * place_out])
        )
        stores[-1].start()
    wait_bytes(send_a.at[pl.ds(0, tm_size - 1)], send_sem.at[0])
    wait_bytes(send_f.at[pl.ds(0, tm_size - 1)], send_sem.at[1])
    wait_bytes(send_c.at[pl.ds(0, tm_size - 1)], send_sem.at[3])

    @pl.when(adder == dp)
    def _():
        wait_bytes(send_r.at[pl.ds(0, tm_size - 1)], send_sem.at[2])

    @pl.when(adder != dp)
    def _():
        wait_bytes(send_r, send_sem.at[2])

    wait_bytes(recv_g.at[pl.ds(0, tm_size - per)], send_sem.at[4])
    for store in stores:
        store.wait()
    own_g.wait()
    wait_bytes(recv_g.at[pl.ds(0, tm_size - per)], recv_sem.at[4])


def finish(
    layer_in, gradw_in, third_hbm, layer_hbm, gradw_hbm, fgrad_hbm, clips, third, turned, load_sem, store_sem
):
    channels, samples = turned.shape[1], turned.shape[0]
    loads = [
        pltpu.make_async_copy(third_hbm, third, load_sem.at[2]),
        pltpu.make_async_copy(layer_in, clips.at[0], load_sem.at[0]),
        pltpu.make_async_copy(gradw_in, clips.at[1], load_sem.at[1]),
    ]
    stores = [
        pltpu.make_async_copy(turned, fgrad_hbm, store_sem.at[2]),
        pltpu.make_async_copy(clips.at[0], layer_hbm, store_sem.at[0]),
        pltpu.make_async_copy(clips.at[1], gradw_hbm, store_sem.at[1]),
    ]
    for load in loads:
        load.start()
    loads[0].wait()
    turned[...] = third[...].reshape(channels, samples).T
    stores[0].start()
    for place in (1, 2):
        loads[place].wait()
        stores[place].start()
    for store in stores:
        store.wait()


def local(waveform, speaker_ids, speaker_table, stencil_taps, skip_gain, filters, cotangent):
    tm_size, dp_size = lax.axis_size("tm"), lax.axis_size("dp")
    samples, channels = filters.shape
    per = tm_size // dp_size
    rows = tm_size * PACK
    table = make_table(tm_size, samples)
    anywhere = pl.BlockSpec(memory_space=pl.ANY)
    block = jax.ShapeDtypeStruct((samples, channels), F32)
    pieces = jax.ShapeDtypeStruct((tm_size, PACK, samples), F32)
    received = pl.pallas_call(
        functools.partial(kernel, tm_size, dp_size),
        out_shape=[block, block, pieces],
        in_specs=[anywhere] * 8,
        out_specs=[anywhere] * 3,
        scratch_shapes=[
            pltpu.SMEM((1,), jnp.int32),
            pltpu.VMEM((samples, channels), BF16),
            pltpu.VMEM((samples, channels), BF16),
            pltpu.VMEM((samples, channels), F32),
            pltpu.VMEM(stencil_taps.shape, F32),
            pltpu.VMEM((1, channels), F32),
            pltpu.VMEM((speaker_table.shape[0] // ROWS16, ROWS16, channels), BF16),
            pltpu.VMEM(table.shape, F32),
            *[pltpu.VMEM((rows, rows), BF16)] * 4,
            pltpu.VMEM((2 * samples, 2 * samples), BF16),
            pltpu.VMEM((2 * samples, 2 * samples), BF16),
            pltpu.VMEM((tm_size, 2 * PACK, samples), BF16),
            pltpu.VMEM((tm_size, 2 * PACK, samples), BF16),
            pltpu.VMEM((tm_size, PACK // 2 + 1, samples), jnp.int32),
            pltpu.VMEM((tm_size, PACK // 2 + 1, samples), jnp.int32),
            pltpu.VMEM((tm_size, PACK + 1, samples), jnp.int32),
            pltpu.VMEM((tm_size, PACK + 1, samples), jnp.int32),
            pltpu.VMEM((2, samples, channels), F32),
            pltpu.VMEM((tm_size, PACK, samples), F32),
            pltpu.VMEM((tm_size, PACK, samples), F32),
            pltpu.VMEM((per, PACK, samples), F32),
            pltpu.SemaphoreType.DMA((11,)),
            pltpu.SemaphoreType.DMA((6,)),
            pltpu.SemaphoreType.DMA((6,)),
            pltpu.SemaphoreType.REGULAR,
        ],
        compiler_params=pltpu.CompilerParams(
            collective_id=0, has_side_effects=True, vmem_limit_bytes=62 * 1024 * 1024
        ),
    )(
        speaker_ids,
        waveform[0],
        cotangent[0],
        filters,
        stencil_taps,
        skip_gain[None],
        speaker_table.reshape(-1, ROWS16, channels),
        jnp.asarray(table),
    )
    layer_out, grad_waveform, filter_grad = pl.pallas_call(
        finish,
        out_shape=[block, block, block],
        in_specs=[anywhere] * 3,
        out_specs=[anywhere] * 3,
        scratch_shapes=[
            pltpu.VMEM((2, samples, channels), F32),
            pltpu.VMEM(pieces.shape, F32),
            pltpu.VMEM((samples, channels), F32),
            pltpu.SemaphoreType.DMA((3,)),
            pltpu.SemaphoreType.DMA((3,)),
        ],
        compiler_params=pltpu.CompilerParams(vmem_limit_bytes=62 * 1024 * 1024),
    )(*received)
    return layer_out[None], grad_waveform[None], filter_grad


def solution(mesh):
    return jax.shard_map(
        local,
        mesh=mesh,
        in_specs=(P("dp", "tm", None), P("dp"), P(), P(), P(), P("tm", None), P("dp", "tm", None)),
        out_specs=(P("dp", "tm", None), P("dp", "tm", None), P("tm", None)),
        check_vma=False,
    )
```

```python
import functools
import math

import jax
import jax.numpy as jnp
import numpy as np
from jax import lax
from jax.experimental import pallas as pl
from jax.experimental.pallas import tpu as pltpu
from jax.sharding import PartitionSpec as P

MESH = pl.DeviceIdType.MESH
F32 = jnp.float32
BF16 = jnp.bfloat16
PACK = 8
ROWS16 = 16


def make_table(blocks, samples):
    total = blocks * samples
    spread = np.eye(PACK)
    block = np.arange(blocks)
    low = np.arange(blocks // 2 + 1)
    angle = 2.0 * math.pi / blocks * (np.outer(low, block) % blocks)
    forward = np.concatenate([np.cos(angle), -np.sin(angle)[1:-1]])
    weight = np.where((low == 0) | (low == blocks // 2), 1.0, 2.0)[:, None] / total
    backward = np.concatenate([weight * np.cos(angle), (weight * np.sin(angle))[1:-1]]).T
    inner = np.arange(samples)
    angle = 2.0 * math.pi / samples * (np.outer(inner, inner) % samples)
    right = np.block([[np.cos(angle), -np.sin(angle)], [np.sin(angle), np.cos(angle)]])
    turn = np.repeat(2.0 * math.pi / total * np.outer(low, inner), PACK, axis=0)
    turn = np.concatenate([np.cos(turn), np.sin(turn)], axis=1)
    parts = [np.kron(forward, spread), np.kron(backward, spread), right, turn]
    wide = max(part.shape[1] for part in parts)
    parts = [np.pad(part, ((0, 0), (0, wide - part.shape[1]))) for part in parts]
    return np.concatenate(parts).astype(np.float32)


def split(array):
    high = array.astype(BF16)
    return high, (array - high.astype(F32)).astype(BF16)


def dot(a, b):
    return jnp.dot(a, b, preferred_element_type=F32)


def quantize(field):
    peak = jnp.max(jnp.abs(field), axis=2, keepdims=True)
    power = jnp.floor(4.0 * jnp.log2(32000.0 / jnp.maximum(peak, 1e-30)))
    return jnp.round(field * jnp.exp2(0.25 * power)).astype(jnp.int32), power + 512.0


def step_size(power):
    return jnp.exp2(0.25 * (512.0 - power))


def diagonal(blocks, lanes):
    shape = (blocks, PACK, lanes)
    return lax.broadcasted_iota(jnp.int32, shape, 1) == lax.broadcasted_iota(jnp.int32, shape, 2)


def lay_out(power, lanes):
    spread = jnp.where(diagonal(power.shape[0], lanes), power, 0.0)
    return jnp.sum(spread, axis=1, keepdims=True).astype(jnp.int32)


def stand_up(row):
    spread = jnp.where(diagonal(row.shape[0], row.shape[2]), row.astype(F32), 0.0)
    return jnp.sum(spread, axis=2, keepdims=True)


def pair(high, low):
    return (high << 16) | (low & 0xFFFF)


def first_of(word):
    return (word >> 16).astype(F32)


def second_of(word):
    return ((word << 16) >> 16).astype(F32)


def encode_one(field, target):
    steps, power = quantize(field)
    half = PACK // 2
    target[:, :half] = pair(steps, pltpu.roll(steps, half, 1))[:, :half]
    target[:, half:] = lay_out(power, field.shape[2])


def decode_one(source):
    half = PACK // 2
    words = source[:, :half]
    power = stand_up(source[:, half:])
    return jnp.concatenate([first_of(words), second_of(words)], axis=1) * step_size(power)


def encode_two(first, second, target):
    first_steps, first_power = quantize(first)
    second_steps, second_power = quantize(second)
    target[:, :PACK] = pair(first_steps, second_steps)
    target[:, PACK:] = lay_out(first_power + 1024.0 * second_power, first.shape[2])


def decode_two(source):
    words = source[:, :PACK]
    powers = stand_up(source[:, PACK:]).astype(jnp.int32)
    first_power = (powers & 1023).astype(F32)
    second_power = (powers >> 10).astype(F32)
    return first_of(words) * step_size(first_power), second_of(words) * step_size(second_power)


def adders(size):
    return [4, 2, 5, 3, 6, 0, 7, 1] if size == 8 else list(range(size))


def pick(values, index):
    return sum(jnp.where(index == place, int(value), 0) for place, value in enumerate(values))


def far_first(step, size):
    shift = lax.div(step + 1, 2)
    return lax.rem(size + size // 2 + jnp.where(lax.rem(step, 2) == 1, -shift, shift), size)


def stencil(field, taps):
    lanes = field.shape[2]
    lane = lax.broadcasted_iota(jnp.int32, field.shape, 2)
    edge = jnp.zeros((1,) + field.shape[1:], F32)
    turned = pltpu.roll(field, 1, 2)
    before = jnp.where(lane == 0, jnp.concatenate([edge, turned[:-1]], axis=0), turned)
    turned = pltpu.roll(field, lanes - 1, 2)
    after = jnp.where(lane == lanes - 1, jnp.concatenate([turned[1:], edge], axis=0), turned)
    return taps[0] * before + taps[1] * field + taps[2] * after


def kernel(
    tm_size,
    dp_size,
    ids_hbm,
    wave_hbm,
    cot_hbm,
    filt_hbm,
    taps_hbm,
    gain_hbm,
    speakers_hbm,
    table_hbm,
    layer_hbm,
    gradw_hbm,
    recv_g,
    ids,
    wave_ref,
    cot_ref,
    filt_ref,
    taps_ref,
    gain_ref,
    speakers,
    table,
    lh,
    ll,
    bh,
    bl,
    rh,
    rl,
    send_a,
    recv_a,
    send_f,
    recv_f,
    send_c,
    recv_c,
    turned,
    send_r,
    recv_r,
    send_g,
    local_sem,
    send_sem,
    recv_sem,
    plane_sem,
):
    dp = lax.axis_index("dp")
    tm = lax.axis_index("tm")
    per = tm_size // dp_size
    place = lax.div(tm, dp_size)
    column_at = lax.rem(tm, dp_size)
    samples = wave_ref.shape[0]
    channels = wave_ref.shape[1]
    rows = tm_size * PACK

    pairs = [
        (wave_hbm, wave_ref),
        (cot_hbm, cot_ref),
        (filt_hbm, filt_ref),
        (table_hbm, table),
        (taps_hbm, taps_ref),
        (gain_hbm, gain_ref),
        (ids_hbm, ids),
        (speakers_hbm, speakers),
    ]
    loads = [
        pltpu.make_async_copy(source, target, local_sem.at[slot])
        for slot, (source, target) in enumerate(pairs)
    ]

    for load in loads[:3]:
        load.start()

    barrier = pltpu.get_barrier_semaphore()

    def tm_peer(step):
        far = far_first(lax.div(step, per), dp_size)
        across = far_first(lax.rem(step, per), per)
        return lax.rem(place + across, per) * dp_size + lax.rem(column_at + far, dp_size)

    def dp_peer(step):
        return lax.rem(dp + far_first(step, dp_size), dp_size)

    @pl.loop(0, tm_size - 1)
    def _(step):
        pl.semaphore_signal(barrier, inc=1, device_id=(dp, tm_peer(step)), device_id_type=MESH)

    @pl.loop(0, dp_size - 1)
    def _(step):
        pl.semaphore_signal(barrier, inc=1, device_id=(dp_peer(step), tm), device_id_type=MESH)

    def wait_bytes(like, sem):
        pltpu.make_async_copy(like, like, sem).wait()

    def exchange(source, target, which):
        @pl.loop(0, tm_size - 1)
        def _(step):
            peer = tm_peer(step)
            pltpu.make_async_remote_copy(
                src_ref=source.at[peer],
                dst_ref=target.at[tm],
                send_sem=send_sem.at[which],
                recv_sem=recv_sem.at[which],
                device_id=(dp, peer),
                device_id_type=MESH,
            ).start()

    def to_blocks(field):
        return field.reshape(tm_size, PACK, samples)

    loads[0].wait()
    wave_t = to_blocks(wave_ref[...].astype(F32).T)
    loads[1].wait()
    cot_t = to_blocks(cot_ref[...].astype(F32).T)
    send_a[...] = jnp.concatenate([wave_t, cot_t], axis=1).astype(BF16)
    pl.semaphore_wait(barrier, tm_size - 1 + dp_size - 1)
    exchange(send_a, recv_a, 0)
    recv_a[tm] = send_a[tm]

    adder = pick(adders(dp_size), lax.div(tm, per))
    share = pick(np.argsort(adders(dp_size)), dp)

    @pl.when(adder == dp)
    def _():
        @pl.loop(0, dp_size - 1)
        def _(step):
            pl.semaphore_signal(plane_sem, inc=1, device_id=(dp_peer(step), tm), device_id_type=MESH)

    for load in loads[3:]:
        load.start()
    for load in loads[3:]:
        load.wait()
    lh[...], ll[...] = split(table[:rows, :rows])
    bh[...], bl[...] = split(table[rows : 2 * rows, :rows])
    rh[...], rl[...] = split(table[2 * rows : 2 * rows + 2 * samples, : 2 * samples])
    tc = table[2 * rows + 2 * samples :, :samples]
    ts = table[2 * rows + 2 * samples :, samples : 2 * samples]
    loads[2].wait()
    encode_one(to_blocks(filt_ref[...].T), send_f)
    exchange(send_f, recv_f, 1)
    recv_f[tm] = send_f[tm]

    lane = lax.broadcasted_iota(jnp.int32, (PACK, channels), 1)
    row = lax.broadcasted_iota(jnp.int32, (PACK, channels), 0)
    mine = lane == tm * PACK + row

    def column(vector):
        return jnp.sum(jnp.where(mine, vector, 0.0), axis=1, keepdims=True)

    speaker = ids[0]
    group = speakers[lax.div(speaker, ROWS16)]
    picked = lax.broadcasted_iota(jnp.int32, (ROWS16, channels), 0) == lax.rem(speaker, ROWS16)
    speaker_row = jnp.sum(jnp.where(picked, group.astype(F32), 0.0), axis=0, keepdims=True)
    scale = column(speaker_row)
    taps = [column(taps_ref[place : place + 1, :]) for place in range(3)]
    gain = column(gain_ref[...])

    def right_mix(field):
        high, low = split(field)
        return dot(high, rh[...]) + (dot(high, rl[...]) + dot(low, rh[...]))

    def twiddle(real, imag):
        return real * tc + imag * ts, imag * tc - real * ts

    half_rows = (tm_size // 2 + 1) * PACK

    def forward(mixed):
        count = mixed.shape[1] // samples
        blank = jnp.zeros((PACK, samples), F32)
        turned = []
        for field in range(count):
            part = mixed[:, field * samples : (field + 1) * samples]
            imag = jnp.concatenate([blank, part[half_rows:], blank], axis=0)
            turned.append(jnp.concatenate(twiddle(part[:half_rows], imag), axis=1))
        result = right_mix(jnp.concatenate(turned, axis=0))
        parts = [result[field * half_rows : (field + 1) * half_rows] for field in range(count)]
        return [(part[:, :samples], part[:, samples:]) for part in parts]

    def backward(spectra):
        packed = [jnp.concatenate([real, -imag], axis=1) for real, imag in spectra]
        inner = right_mix(jnp.concatenate(packed, axis=0))
        turned = []
        for field in range(len(spectra)):
            part = inner[field * half_rows : (field + 1) * half_rows]
            real, imag = twiddle(part[:, :samples], part[:, samples:])
            turned.append(jnp.concatenate([real, imag[PACK:-PACK]], axis=0))
        high, low = split(jnp.concatenate(turned, axis=1))
        return dot(bh[...], high) + (dot(bl[...], high) + dot(bh[...], low))

    wait_bytes(recv_a.at[pl.ds(0, tm_size - 1)], recv_sem.at[0])
    both = recv_a[...].astype(F32)
    value = stencil(both[:, :PACK], taps) * scale
    grad = both[:, PACK:]
    value_high, value_low = split(value.reshape(rows, samples))
    high = jnp.concatenate([value_high, grad.reshape(rows, samples).astype(BF16)], axis=1)
    mixed = dot(lh[...], high) + dot(ll[...], high)
    mixed_value = mixed[:, :samples] + dot(lh[...], value_low)
    mixed = jnp.concatenate([mixed_value, mixed[:, samples:]], axis=1)
    (vr, vi), (gr, gi) = forward(mixed)
    send_r[...] = to_blocks(backward([(vr * gr + vi * gi, vr * gi - vi * gr)]))

    @pl.when(adder != dp)
    def _():
        pl.semaphore_wait(plane_sem, 1)

    slot = dp * per + lax.rem(tm, per)

    def send_partial(block):
        pltpu.make_async_remote_copy(
            src_ref=send_r.at[block],
            dst_ref=recv_r.at[slot],
            send_sem=send_sem.at[2],
            recv_sem=recv_sem.at[2],
            device_id=(adder, block),
            device_id_type=MESH,
        ).start()

    @pl.when(jnp.logical_not((tm == 0) & (adder == dp)))
    def _():
        send_partial(0)

    @pl.loop(0, tm_size)
    def _(step):
        block = lax.rem(place + far_first(lax.rem(step, per), per), per) * dp_size + lax.div(step, per)

        @pl.when((block != 0) & jnp.logical_not((block == tm) & (adder == dp)))
        def _():
            send_partial(block)

    @pl.when(adder == dp)
    def _():
        recv_r[slot] = send_r[tm]

    wait_bytes(recv_f.at[pl.ds(0, tm_size - 1)], recv_sem.at[1])
    high, low = split(decode_one(recv_f).reshape(rows, samples))
    ((fr, fi),) = forward(dot(lh[...], high) + (dot(ll[...], high) + dot(lh[...], low)))
    results = backward(
        [
            (vr * fr - vi * fi, vr * fi + vi * fr),
            (gr * fr + gi * fi, gi * fr - gr * fi),
        ]
    )
    convolved, correlated = results[:, :samples], results[:, samples:]
    layer = to_blocks(convolved) + gain * value
    middle = (to_blocks(correlated) + gain * grad) * scale
    encode_two(layer, stencil(middle, taps[::-1]), send_c)
    @pl.loop(0, tm_size)
    def _(step):
        peer = lax.rem(place + far_first(lax.rem(step, per), per), per) * dp_size + lax.div(step, per)

        @pl.when(peer != tm)
        def _():
            pltpu.make_async_remote_copy(
                src_ref=send_c.at[peer],
                dst_ref=recv_c.at[tm],
                send_sem=send_sem.at[3],
                recv_sem=recv_sem.at[3],
                device_id=(dp, peer),
                device_id_type=MESH,
            ).start()

    recv_c[tm] = send_c[tm]

    @pl.when(adder == dp)
    def _():
        wait_bytes(recv_r.at[pl.ds(0, tm_size - 1)], recv_sem.at[2])

    @pl.when(adder != dp)
    def _():
        wait_bytes(recv_r, recv_sem.at[2])

    send_g[...] = jnp.sum(recv_r[...].reshape(dp_size, per, PACK, samples), axis=0)
    summed = recv_g.at[pl.ds(share * per, per)]

    @pl.loop(0, dp_size - 1)
    def _(step):
        pltpu.make_async_remote_copy(
            src_ref=send_g,
            dst_ref=summed,
            send_sem=send_sem.at[4],
            recv_sem=recv_sem.at[4],
            device_id=(dp_peer(step), tm),
            device_id_type=MESH,
        ).start()

    own_g = pltpu.make_async_copy(send_g, summed, local_sem.at[9])
    own_g.start()
    wait_bytes(recv_c.at[pl.ds(0, tm_size - 1)], recv_sem.at[3])
    stores = []
    for place_out, (field, target) in enumerate(zip(decode_two(recv_c), (layer_hbm, gradw_hbm))):
        turned[place_out] = field.reshape(channels, samples).T
        stores.append(
            pltpu.make_async_copy(turned.at[place_out], target, local_sem.at[8 + 2 * place_out])
        )
        stores[-1].start()
    wait_bytes(send_a.at[pl.ds(0, tm_size - 1)], send_sem.at[0])
    wait_bytes(send_f.at[pl.ds(0, tm_size - 1)], send_sem.at[1])
    wait_bytes(send_c.at[pl.ds(0, tm_size - 1)], send_sem.at[3])

    @pl.when(adder == dp)
    def _():
        wait_bytes(send_r.at[pl.ds(0, tm_size - 1)], send_sem.at[2])

    @pl.when(adder != dp)
    def _():
        wait_bytes(send_r, send_sem.at[2])

    wait_bytes(recv_g.at[pl.ds(0, tm_size - per)], send_sem.at[4])
    for store in stores:
        store.wait()
    own_g.wait()
    wait_bytes(recv_g.at[pl.ds(0, tm_size - per)], recv_sem.at[4])


def finish(
    layer_in, gradw_in, third_hbm, layer_hbm, gradw_hbm, fgrad_hbm, clips, third, turned, load_sem, store_sem
):
    channels, samples = turned.shape[1], turned.shape[0]
    loads = [
        pltpu.make_async_copy(third_hbm, third, load_sem.at[2]),
        pltpu.make_async_copy(layer_in, clips.at[0], load_sem.at[0]),
        pltpu.make_async_copy(gradw_in, clips.at[1], load_sem.at[1]),
    ]
    stores = [
        pltpu.make_async_copy(turned, fgrad_hbm, store_sem.at[2]),
        pltpu.make_async_copy(clips.at[0], layer_hbm, store_sem.at[0]),
        pltpu.make_async_copy(clips.at[1], gradw_hbm, store_sem.at[1]),
    ]
    for load in loads:
        load.start()
    loads[0].wait()
    turned[...] = third[...].reshape(channels, samples).T
    stores[0].start()
    for place in (1, 2):
        loads[place].wait()
        stores[place].start()
    for store in stores:
        store.wait()


def local(waveform, speaker_ids, speaker_table, stencil_taps, skip_gain, filters, cotangent):
    tm_size, dp_size = lax.axis_size("tm"), lax.axis_size("dp")
    samples, channels = filters.shape
    per = tm_size // dp_size
    rows = tm_size * PACK
    table = make_table(tm_size, samples)
    anywhere = pl.BlockSpec(memory_space=pl.ANY)
    block = jax.ShapeDtypeStruct((samples, channels), F32)
    pieces = jax.ShapeDtypeStruct((tm_size, PACK, samples), F32)
    received = pl.pallas_call(
        functools.partial(kernel, tm_size, dp_size),
        out_shape=[block, block, pieces],
        in_specs=[anywhere] * 8,
        out_specs=[anywhere] * 3,
        scratch_shapes=[
            pltpu.SMEM((1,), jnp.int32),
            pltpu.VMEM((samples, channels), BF16),
            pltpu.VMEM((samples, channels), BF16),
            pltpu.VMEM((samples, channels), F32),
            pltpu.VMEM(stencil_taps.shape, F32),
            pltpu.VMEM((1, channels), F32),
            pltpu.VMEM((speaker_table.shape[0] // ROWS16, ROWS16, channels), BF16),
            pltpu.VMEM(table.shape, F32),
            *[pltpu.VMEM((rows, rows), BF16)] * 4,
            pltpu.VMEM((2 * samples, 2 * samples), BF16),
            pltpu.VMEM((2 * samples, 2 * samples), BF16),
            pltpu.VMEM((tm_size, 2 * PACK, samples), BF16),
            pltpu.VMEM((tm_size, 2 * PACK, samples), BF16),
            pltpu.VMEM((tm_size, PACK // 2 + 1, samples), jnp.int32),
            pltpu.VMEM((tm_size, PACK // 2 + 1, samples), jnp.int32),
            pltpu.VMEM((tm_size, PACK + 1, samples), jnp.int32),
            pltpu.VMEM((tm_size, PACK + 1, samples), jnp.int32),
            pltpu.VMEM((2, samples, channels), F32),
            pltpu.VMEM((tm_size, PACK, samples), F32),
            pltpu.VMEM((tm_size, PACK, samples), F32),
            pltpu.VMEM((per, PACK, samples), F32),
            pltpu.SemaphoreType.DMA((11,)),
            pltpu.SemaphoreType.DMA((6,)),
            pltpu.SemaphoreType.DMA((6,)),
            pltpu.SemaphoreType.REGULAR,
        ],
        compiler_params=pltpu.CompilerParams(
            collective_id=0, has_side_effects=True, vmem_limit_bytes=62 * 1024 * 1024
        ),
    )(
        speaker_ids,
        waveform[0],
        cotangent[0],
        filters,
        stencil_taps,
        skip_gain[None],
        speaker_table.reshape(-1, ROWS16, channels),
        jnp.asarray(table),
    )
    layer_out, grad_waveform, filter_grad = pl.pallas_call(
        finish,
        out_shape=[block, block, block],
        in_specs=[anywhere] * 3,
        out_specs=[anywhere] * 3,
        scratch_shapes=[
            pltpu.VMEM((2, samples, channels), F32),
            pltpu.VMEM(pieces.shape, F32),
            pltpu.VMEM((samples, channels), F32),
            pltpu.SemaphoreType.DMA((3,)),
            pltpu.SemaphoreType.DMA((3,)),
        ],
        compiler_params=pltpu.CompilerParams(vmem_limit_bytes=62 * 1024 * 1024),
    )(*received)
    return layer_out[None], grad_waveform[None], filter_grad


def solution(mesh):
    return jax.shard_map(
        local,
        mesh=mesh,
        in_specs=(P("dp", "tm", None), P("dp"), P(), P(), P(), P("tm", None), P("dp", "tm", None)),
        out_specs=(P("dp", "tm", None), P("dp", "tm", None), P("tm", None)),
        check_vma=False,
    )
```

```python
import functools
import math

import jax
import jax.numpy as jnp
import numpy as np
from jax import lax
from jax.experimental import pallas as pl
from jax.experimental.pallas import tpu as pltpu
from jax.sharding import PartitionSpec as P

MESH = pl.DeviceIdType.MESH
F32 = jnp.float32
BF16 = jnp.bfloat16
PACK = 8
ROWS16 = 16


def make_table(blocks, samples):
    total = blocks * samples
    spread = np.eye(PACK)
    block = np.arange(blocks)
    low = np.arange(blocks // 2 + 1)
    angle = 2.0 * math.pi / blocks * (np.outer(low, block) % blocks)
    forward = np.concatenate([np.cos(angle), -np.sin(angle)[1:-1]])
    weight = np.where((low == 0) | (low == blocks // 2), 1.0, 2.0)[:, None] / total
    backward = np.concatenate([weight * np.cos(angle), (weight * np.sin(angle))[1:-1]]).T
    inner = np.arange(samples)
    angle = 2.0 * math.pi / samples * (np.outer(inner, inner) % samples)
    right = np.block([[np.cos(angle), -np.sin(angle)], [np.sin(angle), np.cos(angle)]])
    turn = np.repeat(2.0 * math.pi / total * np.outer(low, inner), PACK, axis=0)
    turn = np.concatenate([np.cos(turn), np.sin(turn)], axis=1)
    parts = [np.kron(forward, spread), np.kron(backward, spread), right, turn]
    wide = max(part.shape[1] for part in parts)
    parts = [np.pad(part, ((0, 0), (0, wide - part.shape[1]))) for part in parts]
    return np.concatenate(parts).astype(np.float32)


def split(array):
    high = array.astype(BF16)
    return high, (array - high.astype(F32)).astype(BF16)


def dot(a, b):
    return jnp.dot(a, b, preferred_element_type=F32)


def quantize(field):
    peak = jnp.max(jnp.abs(field), axis=2, keepdims=True)
    power = jnp.floor(4.0 * jnp.log2(32000.0 / jnp.maximum(peak, 1e-30)))
    return jnp.round(field * jnp.exp2(0.25 * power)).astype(jnp.int32), power + 512.0


def step_size(power):
    return jnp.exp2(0.25 * (512.0 - power))


def diagonal(blocks, lanes):
    shape = (blocks, PACK, lanes)
    return lax.broadcasted_iota(jnp.int32, shape, 1) == lax.broadcasted_iota(jnp.int32, shape, 2)


def lay_out(power, lanes):
    spread = jnp.where(diagonal(power.shape[0], lanes), power, 0.0)
    return jnp.sum(spread, axis=1, keepdims=True).astype(jnp.int32)


def stand_up(row):
    spread = jnp.where(diagonal(row.shape[0], row.shape[2]), row.astype(F32), 0.0)
    return jnp.sum(spread, axis=2, keepdims=True)


def pair(high, low):
    return (high << 16) | (low & 0xFFFF)


def first_of(word):
    return (word >> 16).astype(F32)


def second_of(word):
    return ((word << 16) >> 16).astype(F32)


def encode_one(field, target):
    steps, power = quantize(field)
    half = PACK // 2
    target[:, :half] = pair(steps, pltpu.roll(steps, half, 1))[:, :half]
    target[:, half:] = lay_out(power, field.shape[2])


def decode_one(source):
    half = PACK // 2
    words = source[:, :half]
    power = stand_up(source[:, half:])
    return jnp.concatenate([first_of(words), second_of(words)], axis=1) * step_size(power)


def encode_two(first, second, target):
    first_steps, first_power = quantize(first)
    second_steps, second_power = quantize(second)
    target[:, :PACK] = pair(first_steps, second_steps)
    target[:, PACK:] = lay_out(first_power + 1024.0 * second_power, first.shape[2])


def decode_two(source):
    words = source[:, :PACK]
    powers = stand_up(source[:, PACK:]).astype(jnp.int32)
    first_power = (powers & 1023).astype(F32)
    second_power = (powers >> 10).astype(F32)
    return first_of(words) * step_size(first_power), second_of(words) * step_size(second_power)


def adders(size):
    return [4, 2, 5, 3, 6, 0, 7, 1] if size == 8 else list(range(size))


def pick(values, index):
    return sum(jnp.where(index == place, int(value), 0) for place, value in enumerate(values))


def far_first(step, size):
    shift = lax.div(step + 1, 2)
    return lax.rem(size + size // 2 + jnp.where(lax.rem(step, 2) == 1, -shift, shift), size)


def stencil(field, taps):
    lanes = field.shape[2]
    lane = lax.broadcasted_iota(jnp.int32, field.shape, 2)
    edge = jnp.zeros((1,) + field.shape[1:], F32)
    turned = pltpu.roll(field, 1, 2)
    before = jnp.where(lane == 0, jnp.concatenate([edge, turned[:-1]], axis=0), turned)
    turned = pltpu.roll(field, lanes - 1, 2)
    after = jnp.where(lane == lanes - 1, jnp.concatenate([turned[1:], edge], axis=0), turned)
    return taps[0] * before + taps[1] * field + taps[2] * after


def kernel(
    tm_size,
    dp_size,
    ids_hbm,
    wave_hbm,
    cot_hbm,
    filt_hbm,
    taps_hbm,
    gain_hbm,
    speakers_hbm,
    table_hbm,
    layer_ref,
    gradw_ref,
    recv_g,
    ids,
    wave_ref,
    cot_ref,
    filt_ref,
    taps_ref,
    gain_ref,
    speakers,
    table,
    lh,
    ll,
    bh,
    bl,
    rh,
    rl,
    send_a,
    recv_a,
    send_f,
    recv_f,
    send_c,
    recv_c,
    send_r,
    recv_r,
    send_g,
    local_sem,
    send_sem,
    recv_sem,
    plane_sem,
):
    dp = lax.axis_index("dp")
    tm = lax.axis_index("tm")
    per = tm_size // dp_size
    place = lax.div(tm, dp_size)
    column_at = lax.rem(tm, dp_size)
    samples = wave_ref.shape[0]
    channels = wave_ref.shape[1]
    rows = tm_size * PACK

    pairs = [
        (wave_hbm, wave_ref),
        (cot_hbm, cot_ref),
        (filt_hbm, filt_ref),
        (table_hbm, table),
        (taps_hbm, taps_ref),
        (gain_hbm, gain_ref),
        (ids_hbm, ids),
        (speakers_hbm, speakers),
    ]
    loads = [
        pltpu.make_async_copy(source, target, local_sem.at[slot])
        for slot, (source, target) in enumerate(pairs)
    ]

    for load in loads[:3]:
        load.start()

    barrier = pltpu.get_barrier_semaphore()

    def tm_peer(step):
        far = far_first(lax.div(step, per), dp_size)
        across = far_first(lax.rem(step, per), per)
        return lax.rem(place + across, per) * dp_size + lax.rem(column_at + far, dp_size)

    def dp_peer(step):
        return lax.rem(dp + far_first(step, dp_size), dp_size)

    @pl.loop(0, tm_size - 1)
    def _(step):
        pl.semaphore_signal(barrier, inc=1, device_id=(dp, tm_peer(step)), device_id_type=MESH)

    @pl.loop(0, dp_size - 1)
    def _(step):
        pl.semaphore_signal(barrier, inc=1, device_id=(dp_peer(step), tm), device_id_type=MESH)

    def wait_bytes(like, sem):
        pltpu.make_async_copy(like, like, sem).wait()

    def exchange(source, target, which):
        @pl.loop(0, tm_size - 1)
        def _(step):
            peer = tm_peer(step)
            pltpu.make_async_remote_copy(
                src_ref=source.at[peer],
                dst_ref=target.at[tm],
                send_sem=send_sem.at[which],
                recv_sem=recv_sem.at[which],
                device_id=(dp, peer),
                device_id_type=MESH,
            ).start()

    def to_blocks(field):
        return field.reshape(tm_size, PACK, samples)

    loads[0].wait()
    wave_t = to_blocks(wave_ref[...].astype(F32).T)
    loads[1].wait()
    cot_t = to_blocks(cot_ref[...].astype(F32).T)
    send_a[...] = jnp.concatenate([wave_t, cot_t], axis=1).astype(BF16)
    pl.semaphore_wait(barrier, tm_size - 1 + dp_size - 1)
    exchange(send_a, recv_a, 0)
    recv_a[tm] = send_a[tm]

    adder = pick(adders(dp_size), lax.div(tm, per))
    share = pick(np.argsort(adders(dp_size)), dp)

    @pl.when(adder == dp)
    def _():
        @pl.loop(0, dp_size - 1)
        def _(step):
            pl.semaphore_signal(plane_sem, inc=1, device_id=(dp_peer(step), tm), device_id_type=MESH)

    for load in loads[3:]:
        load.start()
    for load in loads[3:]:
        load.wait()
    lh[...], ll[...] = split(table[:rows, :rows])
    bh[...], bl[...] = split(table[rows : 2 * rows, :rows])
    rh[...], rl[...] = split(table[2 * rows : 2 * rows + 2 * samples, : 2 * samples])
    tc = table[2 * rows + 2 * samples :, :samples]
    ts = table[2 * rows + 2 * samples :, samples : 2 * samples]
    loads[2].wait()
    encode_one(to_blocks(filt_ref[...].T), send_f)
    exchange(send_f, recv_f, 1)
    recv_f[tm] = send_f[tm]

    lane = lax.broadcasted_iota(jnp.int32, (PACK, channels), 1)
    row = lax.broadcasted_iota(jnp.int32, (PACK, channels), 0)
    mine = lane == tm * PACK + row

    def column(vector):
        return jnp.sum(jnp.where(mine, vector, 0.0), axis=1, keepdims=True)

    speaker = ids[0]
    group = speakers[lax.div(speaker, ROWS16)]
    picked = lax.broadcasted_iota(jnp.int32, (ROWS16, channels), 0) == lax.rem(speaker, ROWS16)
    speaker_row = jnp.sum(jnp.where(picked, group.astype(F32), 0.0), axis=0, keepdims=True)
    scale = column(speaker_row)
    taps = [column(taps_ref[place : place + 1, :]) for place in range(3)]
    gain = column(gain_ref[...])

    def right_mix(field):
        high, low = split(field)
        return dot(high, rh[...]) + (dot(high, rl[...]) + dot(low, rh[...]))

    def twiddle(real, imag):
        return real * tc + imag * ts, imag * tc - real * ts

    half_rows = (tm_size // 2 + 1) * PACK

    def forward(mixed):
        count = mixed.shape[1] // samples
        blank = jnp.zeros((PACK, samples), F32)
        turned = []
        for field in range(count):
            part = mixed[:, field * samples : (field + 1) * samples]
            imag = jnp.concatenate([blank, part[half_rows:], blank], axis=0)
            turned.append(jnp.concatenate(twiddle(part[:half_rows], imag), axis=1))
        result = right_mix(jnp.concatenate(turned, axis=0))
        parts = [result[field * half_rows : (field + 1) * half_rows] for field in range(count)]
        return [(part[:, :samples], part[:, samples:]) for part in parts]

    def backward(spectra):
        packed = [jnp.concatenate([real, -imag], axis=1) for real, imag in spectra]
        inner = right_mix(jnp.concatenate(packed, axis=0))
        turned = []
        for field in range(len(spectra)):
            part = inner[field * half_rows : (field + 1) * half_rows]
            real, imag = twiddle(part[:, :samples], part[:, samples:])
            turned.append(jnp.concatenate([real, imag[PACK:-PACK]], axis=0))
        high, low = split(jnp.concatenate(turned, axis=1))
        return dot(bh[...], high) + (dot(bl[...], high) + dot(bh[...], low))

    wait_bytes(recv_a.at[pl.ds(0, tm_size - 1)], recv_sem.at[0])
    both = recv_a[...].astype(F32)
    value = stencil(both[:, :PACK], taps) * scale
    grad = both[:, PACK:]
    value_high, value_low = split(value.reshape(rows, samples))
    high = jnp.concatenate([value_high, grad.reshape(rows, samples).astype(BF16)], axis=1)
    mixed = dot(lh[...], high) + dot(ll[...], high)
    mixed_value = mixed[:, :samples] + dot(lh[...], value_low)
    mixed = jnp.concatenate([mixed_value, mixed[:, samples:]], axis=1)
    (vr, vi), (gr, gi) = forward(mixed)
    send_r[...] = to_blocks(backward([(vr * gr + vi * gi, vr * gi - vi * gr)]))

    @pl.when(adder != dp)
    def _():
        pl.semaphore_wait(plane_sem, 1)

    slot = dp * per + lax.rem(tm, per)

    def send_partial(block):
        pltpu.make_async_remote_copy(
            src_ref=send_r.at[block],
            dst_ref=recv_r.at[slot],
            send_sem=send_sem.at[2],
            recv_sem=recv_sem.at[2],
            device_id=(adder, block),
            device_id_type=MESH,
        ).start()

    @pl.when(jnp.logical_not((tm == 0) & (adder == dp)))
    def _():
        send_partial(0)

    @pl.loop(0, tm_size)
    def _(step):
        block = lax.rem(place + far_first(lax.rem(step, per), per), per) * dp_size + lax.div(step, per)

        @pl.when((block != 0) & jnp.logical_not((block == tm) & (adder == dp)))
        def _():
            send_partial(block)

    @pl.when(adder == dp)
    def _():
        recv_r[slot] = send_r[tm]

    wait_bytes(recv_f.at[pl.ds(0, tm_size - 1)], recv_sem.at[1])
    high, low = split(decode_one(recv_f).reshape(rows, samples))
    ((fr, fi),) = forward(dot(lh[...], high) + (dot(ll[...], high) + dot(lh[...], low)))
    results = backward(
        [
            (vr * fr - vi * fi, vr * fi + vi * fr),
            (gr * fr + gi * fi, gi * fr - gr * fi),
        ]
    )
    convolved, correlated = results[:, :samples], results[:, samples:]
    layer = to_blocks(convolved) + gain * value
    middle = (to_blocks(correlated) + gain * grad) * scale
    encode_two(layer, stencil(middle, taps[::-1]), send_c)
    @pl.loop(0, tm_size)
    def _(step):
        peer = lax.rem(place + far_first(lax.rem(step, per), per), per) * dp_size + lax.div(step, per)

        @pl.when(peer != tm)
        def _():
            pltpu.make_async_remote_copy(
                src_ref=send_c.at[peer],
                dst_ref=recv_c.at[tm],
                send_sem=send_sem.at[3],
                recv_sem=recv_sem.at[3],
                device_id=(dp, peer),
                device_id_type=MESH,
            ).start()

    recv_c[tm] = send_c[tm]

    @pl.when(adder == dp)
    def _():
        wait_bytes(recv_r.at[pl.ds(0, tm_size - 1)], recv_sem.at[2])

    @pl.when(adder != dp)
    def _():
        wait_bytes(recv_r, recv_sem.at[2])

    send_g[...] = jnp.sum(recv_r[...].reshape(dp_size, per, PACK, samples), axis=0)
    summed = recv_g.at[pl.ds(share * per, per)]

    @pl.loop(0, dp_size - 1)
    def _(step):
        pltpu.make_async_remote_copy(
            src_ref=send_g,
            dst_ref=summed,
            send_sem=send_sem.at[4],
            recv_sem=recv_sem.at[4],
            device_id=(dp_peer(step), tm),
            device_id_type=MESH,
        ).start()

    own_g = pltpu.make_async_copy(send_g, summed, local_sem.at[9])
    own_g.start()
    wait_bytes(recv_c.at[pl.ds(0, tm_size - 1)], recv_sem.at[3])
    layer, gradw = decode_two(recv_c)
    layer_ref[...] = layer.reshape(channels, samples).T
    gradw_ref[...] = gradw.reshape(channels, samples).T
    wait_bytes(send_a.at[pl.ds(0, tm_size - 1)], send_sem.at[0])
    wait_bytes(send_f.at[pl.ds(0, tm_size - 1)], send_sem.at[1])
    wait_bytes(send_c.at[pl.ds(0, tm_size - 1)], send_sem.at[3])

    @pl.when(adder == dp)
    def _():
        wait_bytes(send_r.at[pl.ds(0, tm_size - 1)], send_sem.at[2])

    @pl.when(adder != dp)
    def _():
        wait_bytes(send_r, send_sem.at[2])

    wait_bytes(recv_g.at[pl.ds(0, tm_size - per)], send_sem.at[4])
    own_g.wait()
    wait_bytes(recv_g.at[pl.ds(0, tm_size - per)], recv_sem.at[4])


def finish(layer_in, gradw_in, third, layer_hbm, gradw_hbm, fgrad_hbm, turned, store_sem):
    channels, samples = turned.shape[1], turned.shape[0]
    stores = [
        pltpu.make_async_copy(layer_in, layer_hbm, store_sem.at[0]),
        pltpu.make_async_copy(gradw_in, gradw_hbm, store_sem.at[1]),
        pltpu.make_async_copy(turned, fgrad_hbm, store_sem.at[2]),
    ]
    stores[0].start()
    stores[1].start()
    turned[...] = third[...].reshape(channels, samples).T
    stores[2].start()
    for store in stores:
        store.wait()


def local(waveform, speaker_ids, speaker_table, stencil_taps, skip_gain, filters, cotangent):
    tm_size, dp_size = lax.axis_size("tm"), lax.axis_size("dp")
    samples, channels = filters.shape
    per = tm_size // dp_size
    rows = tm_size * PACK
    table = make_table(tm_size, samples)
    anywhere = pl.BlockSpec(memory_space=pl.ANY)
    vmem = pl.BlockSpec(memory_space=pltpu.VMEM)
    block = jax.ShapeDtypeStruct((samples, channels), F32)
    pieces = jax.ShapeDtypeStruct((tm_size, PACK, samples), F32)
    received = pl.pallas_call(
        functools.partial(kernel, tm_size, dp_size),
        out_shape=[pltpu.VMEM(block.shape, F32)] * 2 + [pltpu.VMEM(pieces.shape, F32)],
        in_specs=[anywhere] * 8,
        out_specs=[vmem] * 3,
        scratch_shapes=[
            pltpu.SMEM((1,), jnp.int32),
            pltpu.VMEM((samples, channels), BF16),
            pltpu.VMEM((samples, channels), BF16),
            pltpu.VMEM((samples, channels), F32),
            pltpu.VMEM(stencil_taps.shape, F32),
            pltpu.VMEM((1, channels), F32),
            pltpu.VMEM((speaker_table.shape[0] // ROWS16, ROWS16, channels), BF16),
            pltpu.VMEM(table.shape, F32),
            *[pltpu.VMEM((rows, rows), BF16)] * 4,
            pltpu.VMEM((2 * samples, 2 * samples), BF16),
            pltpu.VMEM((2 * samples, 2 * samples), BF16),
            pltpu.VMEM((tm_size, 2 * PACK, samples), BF16),
            pltpu.VMEM((tm_size, 2 * PACK, samples), BF16),
            pltpu.VMEM((tm_size, PACK // 2 + 1, samples), jnp.int32),
            pltpu.VMEM((tm_size, PACK // 2 + 1, samples), jnp.int32),
            pltpu.VMEM((tm_size, PACK + 1, samples), jnp.int32),
            pltpu.VMEM((tm_size, PACK + 1, samples), jnp.int32),
            pltpu.VMEM((tm_size, PACK, samples), F32),
            pltpu.VMEM((tm_size, PACK, samples), F32),
            pltpu.VMEM((per, PACK, samples), F32),
            pltpu.SemaphoreType.DMA((11,)),
            pltpu.SemaphoreType.DMA((6,)),
            pltpu.SemaphoreType.DMA((6,)),
            pltpu.SemaphoreType.REGULAR,
        ],
        compiler_params=pltpu.CompilerParams(
            collective_id=0, has_side_effects=True, vmem_limit_bytes=32 * 1024 * 1024
        ),
    )(
        speaker_ids,
        *[
            pltpu.with_memory_space_constraint(operand, pltpu.HBM)
            for operand in (
                waveform[0],
                cotangent[0],
                filters,
                stencil_taps,
                skip_gain[None],
                speaker_table.reshape(-1, ROWS16, channels),
                jnp.asarray(table),
            )
        ]
    )
    layer_out, grad_waveform, filter_grad = pl.pallas_call(
        finish,
        out_shape=[block, block, block],
        in_specs=[vmem] * 3,
        out_specs=[anywhere] * 3,
        scratch_shapes=[
            pltpu.VMEM((samples, channels), F32),
            pltpu.SemaphoreType.DMA((3,)),
        ],
        compiler_params=pltpu.CompilerParams(vmem_limit_bytes=16 * 1024 * 1024),
    )(*received)
    return layer_out[None], grad_waveform[None], filter_grad


def solution(mesh):
    return jax.shard_map(
        local,
        mesh=mesh,
        in_specs=(P("dp", "tm", None), P("dp"), P(), P(), P(), P("tm", None), P("dp", "tm", None)),
        out_specs=(P("dp", "tm", None), P("dp", "tm", None), P("tm", None)),
        check_vma=False,
    )
```

```python
import functools
import math

import jax
import jax.numpy as jnp
import numpy as np
from jax import lax
from jax.experimental import pallas as pl
from jax.experimental.pallas import tpu as pltpu
from jax.sharding import PartitionSpec as P

MESH = pl.DeviceIdType.MESH
F32 = jnp.float32
BF16 = jnp.bfloat16
PACK = 8
ROWS16 = 16


def make_table(blocks, samples):
    total = blocks * samples
    spread = np.eye(PACK)
    block = np.arange(blocks)
    low = np.arange(blocks // 2 + 1)
    angle = 2.0 * math.pi / blocks * (np.outer(low, block) % blocks)
    forward = np.concatenate([np.cos(angle), -np.sin(angle)[1:-1]])
    weight = np.where((low == 0) | (low == blocks // 2), 1.0, 2.0)[:, None] / total
    backward = np.concatenate([weight * np.cos(angle), (weight * np.sin(angle))[1:-1]]).T
    inner = np.arange(samples)
    angle = 2.0 * math.pi / samples * (np.outer(inner, inner) % samples)
    right = np.block([[np.cos(angle), -np.sin(angle)], [np.sin(angle), np.cos(angle)]])
    turn = np.repeat(2.0 * math.pi / total * np.outer(low, inner), PACK, axis=0)
    turn = np.concatenate([np.cos(turn), np.sin(turn)], axis=1)
    parts = [np.kron(forward, spread), np.kron(backward, spread), right, turn]
    wide = max(part.shape[1] for part in parts)
    parts = [np.pad(part, ((0, 0), (0, wide - part.shape[1]))) for part in parts]
    return np.concatenate(parts).astype(np.float32)


def split(array):
    high = array.astype(BF16)
    return high, (array - high.astype(F32)).astype(BF16)


def dot(a, b):
    return jnp.dot(a, b, preferred_element_type=F32)


def quantize(field):
    peak = jnp.max(jnp.abs(field), axis=2, keepdims=True)
    power = jnp.floor(4.0 * jnp.log2(32000.0 / jnp.maximum(peak, 1e-30)))
    return jnp.round(field * jnp.exp2(0.25 * power)).astype(jnp.int32), power + 512.0


def step_size(power):
    return jnp.exp2(0.25 * (512.0 - power))


def diagonal(blocks, lanes):
    shape = (blocks, PACK, lanes)
    return lax.broadcasted_iota(jnp.int32, shape, 1) == lax.broadcasted_iota(jnp.int32, shape, 2)


def lay_out(power, lanes):
    spread = jnp.where(diagonal(power.shape[0], lanes), power, 0.0)
    return jnp.sum(spread, axis=1, keepdims=True).astype(jnp.int32)


def stand_up(row):
    spread = jnp.where(diagonal(row.shape[0], row.shape[2]), row.astype(F32), 0.0)
    return jnp.sum(spread, axis=2, keepdims=True)


def pair(high, low):
    return (high << 16) | (low & 0xFFFF)


def first_of(word):
    return (word >> 16).astype(F32)


def second_of(word):
    return ((word << 16) >> 16).astype(F32)


def encode_one(field, target):
    steps, power = quantize(field)
    half = PACK // 2
    target[:, :half] = pair(steps, pltpu.roll(steps, half, 1))[:, :half]
    target[:, half:] = lay_out(power, field.shape[2])


def decode_one(source):
    half = PACK // 2
    words = source[:, :half]
    power = stand_up(source[:, half:])
    return jnp.concatenate([first_of(words), second_of(words)], axis=1) * step_size(power)


def encode_two(first, second, target):
    first_steps, first_power = quantize(first)
    second_steps, second_power = quantize(second)
    target[:, :PACK] = pair(first_steps, second_steps)
    target[:, PACK:] = lay_out(first_power + 1024.0 * second_power, first.shape[2])


def decode_two(source):
    words = source[:, :PACK]
    powers = stand_up(source[:, PACK:]).astype(jnp.int32)
    first_power = (powers & 1023).astype(F32)
    second_power = (powers >> 10).astype(F32)
    return first_of(words) * step_size(first_power), second_of(words) * step_size(second_power)


def adders(size):
    return [4, 2, 5, 3, 6, 0, 7, 1] if size == 8 else list(range(size))


def pick(values, index):
    return sum(jnp.where(index == place, int(value), 0) for place, value in enumerate(values))


def far_first(step, size):
    shift = lax.div(step + 1, 2)
    return lax.rem(size + size // 2 + jnp.where(lax.rem(step, 2) == 1, -shift, shift), size)


def stencil(field, taps):
    lanes = field.shape[2]
    lane = lax.broadcasted_iota(jnp.int32, field.shape, 2)
    edge = jnp.zeros((1,) + field.shape[1:], F32)
    turned = pltpu.roll(field, 1, 2)
    before = jnp.where(lane == 0, jnp.concatenate([edge, turned[:-1]], axis=0), turned)
    turned = pltpu.roll(field, lanes - 1, 2)
    after = jnp.where(lane == lanes - 1, jnp.concatenate([turned[1:], edge], axis=0), turned)
    return taps[0] * before + taps[1] * field + taps[2] * after


def kernel(
    tm_size,
    dp_size,
    ids_hbm,
    wave_hbm,
    cot_hbm,
    filt_hbm,
    taps_hbm,
    gain_hbm,
    speakers_hbm,
    table_hbm,
    layer_ref,
    gradw_ref,
    recv_g,
    ids,
    wave_ref,
    cot_ref,
    filt_ref,
    taps_ref,
    gain_ref,
    speakers,
    table,
    lh,
    ll,
    bh,
    bl,
    rh,
    rl,
    send_a,
    recv_a,
    send_f,
    recv_f,
    send_c,
    recv_c,
    send_r,
    recv_r,
    send_g,
    local_sem,
    send_sem,
    recv_sem,
    plane_sem,
):
    dp = lax.axis_index("dp")
    tm = lax.axis_index("tm")
    per = tm_size // dp_size
    place = lax.div(tm, dp_size)
    column_at = lax.rem(tm, dp_size)
    samples = wave_ref.shape[0]
    channels = wave_ref.shape[1]
    rows = tm_size * PACK

    pairs = [
        (wave_hbm, wave_ref),
        (cot_hbm, cot_ref),
        (filt_hbm, filt_ref),
        (table_hbm, table),
        (taps_hbm, taps_ref),
        (gain_hbm, gain_ref),
        (ids_hbm, ids),
        (speakers_hbm, speakers),
    ]
    loads = [
        pltpu.make_async_copy(source, target, local_sem.at[slot])
        for slot, (source, target) in enumerate(pairs)
    ]

    for load in loads[:3]:
        load.start()

    barrier = pltpu.get_barrier_semaphore()

    def tm_peer(step):
        far = far_first(lax.div(step, per), dp_size)
        across = far_first(lax.rem(step, per), per)
        return lax.rem(place + across, per) * dp_size + lax.rem(column_at + far, dp_size)

    def dp_peer(step):
        return lax.rem(dp + far_first(step, dp_size), dp_size)

    @pl.loop(0, tm_size - 1)
    def _(step):
        pl.semaphore_signal(barrier, inc=1, device_id=(dp, tm_peer(step)), device_id_type=MESH)

    @pl.loop(0, dp_size - 1)
    def _(step):
        pl.semaphore_signal(barrier, inc=1, device_id=(dp_peer(step), tm), device_id_type=MESH)

    def wait_bytes(like, sem):
        pltpu.make_async_copy(like, like, sem).wait()

    def exchange(source, target, which):
        @pl.loop(0, tm_size - 1)
        def _(step):
            peer = tm_peer(lax.rem(step + 15 * lax.rem(dp, 2), tm_size - 1))
            pltpu.make_async_remote_copy(
                src_ref=source.at[peer],
                dst_ref=target.at[tm],
                send_sem=send_sem.at[which],
                recv_sem=recv_sem.at[which],
                device_id=(dp, peer),
                device_id_type=MESH,
            ).start()

    def to_blocks(field):
        return field.reshape(tm_size, PACK, samples)

    loads[0].wait()
    wave_t = to_blocks(wave_ref[...].astype(F32).T)
    loads[1].wait()
    cot_t = to_blocks(cot_ref[...].astype(F32).T)
    send_a[...] = jnp.concatenate([wave_t, cot_t], axis=1).astype(BF16)
    pl.semaphore_wait(barrier, tm_size - 1 + dp_size - 1)
    exchange(send_a, recv_a, 0)
    recv_a[tm] = send_a[tm]

    adder = pick(adders(dp_size), lax.div(tm, per))
    share = pick(np.argsort(adders(dp_size)), dp)

    @pl.when(adder == dp)
    def _():
        @pl.loop(0, dp_size - 1)
        def _(step):
            pl.semaphore_signal(plane_sem, inc=1, device_id=(dp_peer(step), tm), device_id_type=MESH)

    for load in loads[3:]:
        load.start()
    for load in loads[3:]:
        load.wait()
    lh[...], ll[...] = split(table[:rows, :rows])
    bh[...], bl[...] = split(table[rows : 2 * rows, :rows])
    rh[...], rl[...] = split(table[2 * rows : 2 * rows + 2 * samples, : 2 * samples])
    tc = table[2 * rows + 2 * samples :, :samples]
    ts = table[2 * rows + 2 * samples :, samples : 2 * samples]
    loads[2].wait()
    encode_one(to_blocks(filt_ref[...].T), send_f)
    exchange(send_f, recv_f, 1)
    recv_f[tm] = send_f[tm]

    lane = lax.broadcasted_iota(jnp.int32, (PACK, channels), 1)
    row = lax.broadcasted_iota(jnp.int32, (PACK, channels), 0)
    mine = lane == tm * PACK + row

    def column(vector):
        return jnp.sum(jnp.where(mine, vector, 0.0), axis=1, keepdims=True)

    speaker = ids[0]
    group = speakers[lax.div(speaker, ROWS16)]
    picked = lax.broadcasted_iota(jnp.int32, (ROWS16, channels), 0) == lax.rem(speaker, ROWS16)
    speaker_row = jnp.sum(jnp.where(picked, group.astype(F32), 0.0), axis=0, keepdims=True)
    scale = column(speaker_row)
    taps = [column(taps_ref[place : place + 1, :]) for place in range(3)]
    gain = column(gain_ref[...])

    def left_mix(table_high, table_low, field):
        high, low = split(field)
        columns = field.shape[1]
        both = dot(table_high[...], jnp.concatenate([high, low], axis=1))
        return both[:, :columns] + (both[:, columns:] + dot(table_low[...], high))

    def right_mix(field):
        high, low = split(field)
        return dot(high, rh[...]) + (dot(high, rl[...]) + dot(low, rh[...]))

    def twiddle(real, imag):
        return real * tc + imag * ts, imag * tc - real * ts

    half_rows = (tm_size // 2 + 1) * PACK

    def forward(mixed):
        count = mixed.shape[1] // samples
        blank = jnp.zeros((PACK, samples), F32)
        turned = []
        for field in range(count):
            part = mixed[:, field * samples : (field + 1) * samples]
            imag = jnp.concatenate([blank, part[half_rows:], blank], axis=0)
            turned.append(jnp.concatenate(twiddle(part[:half_rows], imag), axis=1))
        result = right_mix(jnp.concatenate(turned, axis=0))
        parts = [result[field * half_rows : (field + 1) * half_rows] for field in range(count)]
        return [(part[:, :samples], part[:, samples:]) for part in parts]

    def backward(spectra):
        packed = [jnp.concatenate([real, -imag], axis=1) for real, imag in spectra]
        inner = right_mix(jnp.concatenate(packed, axis=0))
        turned = []
        for field in range(len(spectra)):
            part = inner[field * half_rows : (field + 1) * half_rows]
            real, imag = twiddle(part[:, :samples], part[:, samples:])
            turned.append(jnp.concatenate([real, imag[PACK:-PACK]], axis=0))
        return left_mix(bh, bl, jnp.concatenate(turned, axis=1))

    wait_bytes(recv_a.at[pl.ds(0, tm_size - 1)], recv_sem.at[0])
    both = recv_a[...].astype(F32)
    value = stencil(both[:, :PACK], taps) * scale
    grad = both[:, PACK:]
    value_high, value_low = split(value.reshape(rows, samples))
    high = jnp.concatenate([value_high, grad.reshape(rows, samples).astype(BF16)], axis=1)
    mixed = dot(lh[...], high) + dot(ll[...], high)
    mixed_value = mixed[:, :samples] + dot(lh[...], value_low)
    mixed = jnp.concatenate([mixed_value, mixed[:, samples:]], axis=1)
    (vr, vi), (gr, gi) = forward(mixed)
    send_r[...] = to_blocks(backward([(vr * gr + vi * gi, vr * gi - vi * gr)]))

    @pl.when(adder != dp)
    def _():
        pl.semaphore_wait(plane_sem, 1)

    slot = dp * per + lax.rem(tm, per)

    def send_partial(block):
        pltpu.make_async_remote_copy(
            src_ref=send_r.at[block],
            dst_ref=recv_r.at[slot],
            send_sem=send_sem.at[2],
            recv_sem=recv_sem.at[2],
            device_id=(adder, block),
            device_id_type=MESH,
        ).start()

    @pl.when(jnp.logical_not((tm == 0) & (adder == dp)))
    def _():
        send_partial(0)

    @pl.loop(0, tm_size)
    def _(step):
        block = lax.rem(step, per) * dp_size + lax.div(step, per)

        @pl.when((block != 0) & jnp.logical_not((block == tm) & (adder == dp)))
        def _():
            send_partial(block)

    @pl.when(adder == dp)
    def _():
        recv_r[slot] = send_r[tm]

    wait_bytes(recv_f.at[pl.ds(0, tm_size - 1)], recv_sem.at[1])
    ((fr, fi),) = forward(left_mix(lh, ll, decode_one(recv_f).reshape(rows, samples)))
    results = backward(
        [
            (vr * fr - vi * fi, vr * fi + vi * fr),
            (gr * fr + gi * fi, gi * fr - gr * fi),
        ]
    )
    convolved, correlated = results[:, :samples], results[:, samples:]
    layer = to_blocks(convolved) + gain * value
    middle = (to_blocks(correlated) + gain * grad) * scale
    encode_two(layer, stencil(middle, taps[::-1]), send_c)
    @pl.loop(0, tm_size)
    def _(step):
        peer = lax.rem(place + far_first(lax.rem(step, per), per), per) * dp_size + lax.div(step, per)

        @pl.when(peer != tm)
        def _():
            pltpu.make_async_remote_copy(
                src_ref=send_c.at[peer],
                dst_ref=recv_c.at[tm],
                send_sem=send_sem.at[3],
                recv_sem=recv_sem.at[3],
                device_id=(dp, peer),
                device_id_type=MESH,
            ).start()

    recv_c[tm] = send_c[tm]

    @pl.when(adder == dp)
    def _():
        wait_bytes(recv_r.at[pl.ds(0, tm_size - 1)], recv_sem.at[2])

    @pl.when(adder != dp)
    def _():
        wait_bytes(recv_r, recv_sem.at[2])

    send_g[...] = jnp.sum(recv_r[...].reshape(dp_size, per, PACK, samples), axis=0)
    summed = recv_g.at[pl.ds(share * per, per)]

    @pl.loop(0, dp_size - 1)
    def _(step):
        pltpu.make_async_remote_copy(
            src_ref=send_g,
            dst_ref=summed,
            send_sem=send_sem.at[4],
            recv_sem=recv_sem.at[4],
            device_id=(dp_peer(step), tm),
            device_id_type=MESH,
        ).start()

    own_g = pltpu.make_async_copy(send_g, summed, local_sem.at[9])
    own_g.start()
    wait_bytes(recv_c.at[pl.ds(0, tm_size - 1)], recv_sem.at[3])
    layer, gradw = decode_two(recv_c)
    layer_ref[...] = layer.reshape(channels, samples).T
    gradw_ref[...] = gradw.reshape(channels, samples).T
    wait_bytes(send_a.at[pl.ds(0, tm_size - 1)], send_sem.at[0])
    wait_bytes(send_f.at[pl.ds(0, tm_size - 1)], send_sem.at[1])
    wait_bytes(send_c.at[pl.ds(0, tm_size - 1)], send_sem.at[3])

    @pl.when(adder == dp)
    def _():
        wait_bytes(send_r.at[pl.ds(0, tm_size - 1)], send_sem.at[2])

    @pl.when(adder != dp)
    def _():
        wait_bytes(send_r, send_sem.at[2])

    wait_bytes(recv_g.at[pl.ds(0, tm_size - per)], send_sem.at[4])
    own_g.wait()
    wait_bytes(recv_g.at[pl.ds(0, tm_size - per)], recv_sem.at[4])


def finish(layer_in, gradw_in, third, layer_hbm, gradw_hbm, fgrad_hbm, turned, store_sem):
    channels, samples = turned.shape[1], turned.shape[0]
    stores = [
        pltpu.make_async_copy(layer_in, layer_hbm, store_sem.at[0]),
        pltpu.make_async_copy(gradw_in, gradw_hbm, store_sem.at[1]),
        pltpu.make_async_copy(turned, fgrad_hbm, store_sem.at[2]),
    ]
    stores[0].start()
    stores[1].start()
    turned[...] = third[...].reshape(channels, samples).T
    stores[2].start()
    for store in stores:
        store.wait()


def local(waveform, speaker_ids, speaker_table, stencil_taps, skip_gain, filters, cotangent):
    tm_size, dp_size = lax.axis_size("tm"), lax.axis_size("dp")
    samples, channels = filters.shape
    per = tm_size // dp_size
    rows = tm_size * PACK
    table = make_table(tm_size, samples)
    anywhere = pl.BlockSpec(memory_space=pl.ANY)
    vmem = pl.BlockSpec(memory_space=pltpu.VMEM)
    block = jax.ShapeDtypeStruct((samples, channels), F32)
    pieces = jax.ShapeDtypeStruct((tm_size, PACK, samples), F32)
    received = pl.pallas_call(
        functools.partial(kernel, tm_size, dp_size),
        out_shape=[pltpu.VMEM(block.shape, F32)] * 2 + [pltpu.VMEM(pieces.shape, F32)],
        in_specs=[anywhere] * 8,
        out_specs=[vmem] * 3,
        scratch_shapes=[
            pltpu.SMEM((1,), jnp.int32),
            pltpu.VMEM((samples, channels), BF16),
            pltpu.VMEM((samples, channels), BF16),
            pltpu.VMEM((samples, channels), F32),
            pltpu.VMEM(stencil_taps.shape, F32),
            pltpu.VMEM((1, channels), F32),
            pltpu.VMEM((speaker_table.shape[0] // ROWS16, ROWS16, channels), BF16),
            pltpu.VMEM(table.shape, F32),
            *[pltpu.VMEM((rows, rows), BF16)] * 4,
            pltpu.VMEM((2 * samples, 2 * samples), BF16),
            pltpu.VMEM((2 * samples, 2 * samples), BF16),
            pltpu.VMEM((tm_size, 2 * PACK, samples), BF16),
            pltpu.VMEM((tm_size, 2 * PACK, samples), BF16),
            pltpu.VMEM((tm_size, PACK // 2 + 1, samples), jnp.int32),
            pltpu.VMEM((tm_size, PACK // 2 + 1, samples), jnp.int32),
            pltpu.VMEM((tm_size, PACK + 1, samples), jnp.int32),
            pltpu.VMEM((tm_size, PACK + 1, samples), jnp.int32),
            pltpu.VMEM((tm_size, PACK, samples), F32),
            pltpu.VMEM((tm_size, PACK, samples), F32),
            pltpu.VMEM((per, PACK, samples), F32),
            pltpu.SemaphoreType.DMA((11,)),
            pltpu.SemaphoreType.DMA((6,)),
            pltpu.SemaphoreType.DMA((6,)),
            pltpu.SemaphoreType.REGULAR,
        ],
        compiler_params=pltpu.CompilerParams(
            collective_id=0, has_side_effects=True, vmem_limit_bytes=32 * 1024 * 1024
        ),
    )(
        speaker_ids,
        *[
            pltpu.with_memory_space_constraint(operand, pltpu.HBM)
            for operand in (
                waveform[0],
                cotangent[0],
                filters,
                stencil_taps,
                skip_gain[None],
                speaker_table.reshape(-1, ROWS16, channels),
                jnp.asarray(table),
            )
        ]
    )
    layer_out, grad_waveform, filter_grad = pl.pallas_call(
        finish,
        out_shape=[block, block, block],
        in_specs=[vmem] * 3,
        out_specs=[anywhere] * 3,
        scratch_shapes=[
            pltpu.VMEM((samples, channels), F32),
            pltpu.SemaphoreType.DMA((3,)),
        ],
        compiler_params=pltpu.CompilerParams(vmem_limit_bytes=16 * 1024 * 1024),
    )(*received)
    return layer_out[None], grad_waveform[None], filter_grad


def solution(mesh):
    return jax.shard_map(
        local,
        mesh=mesh,
        in_specs=(P("dp", "tm", None), P("dp"), P(), P(), P(), P("tm", None), P("dp", "tm", None)),
        out_specs=(P("dp", "tm", None), P("dp", "tm", None), P("tm", None)),
        check_vma=False,
    )
```

```python
import functools
import math

import jax
import jax.numpy as jnp
import numpy as np
from jax import lax
from jax.experimental import pallas as pl
from jax.experimental.pallas import tpu as pltpu
from jax.sharding import PartitionSpec as P

MESH = pl.DeviceIdType.MESH
F32 = jnp.float32
BF16 = jnp.bfloat16
PACK = 8
ROWS16 = 16


def make_table(blocks, samples):
    total = blocks * samples
    spread = np.eye(PACK)
    block = np.arange(blocks)
    low = np.arange(blocks // 2 + 1)
    angle = 2.0 * math.pi / blocks * (np.outer(low, block) % blocks)
    forward = np.concatenate([np.cos(angle), -np.sin(angle)[1:-1]])
    weight = np.where((low == 0) | (low == blocks // 2), 1.0, 2.0)[:, None] / total
    backward = np.concatenate([weight * np.cos(angle), (weight * np.sin(angle))[1:-1]]).T
    inner = np.arange(samples)
    angle = 2.0 * math.pi / samples * (np.outer(inner, inner) % samples)
    right = np.block([[np.cos(angle), -np.sin(angle)], [np.sin(angle), np.cos(angle)]])
    turn = np.repeat(2.0 * math.pi / total * np.outer(low, inner), PACK, axis=0)
    turn = np.concatenate([np.cos(turn), np.sin(turn)], axis=1)
    parts = [np.kron(forward, spread), np.kron(backward, spread), right, turn]
    wide = max(part.shape[1] for part in parts)
    parts = [np.pad(part, ((0, 0), (0, wide - part.shape[1]))) for part in parts]
    return np.concatenate(parts).astype(np.float32)


def split(array):
    high = array.astype(BF16)
    return high, (array - high.astype(F32)).astype(BF16)


def dot(a, b):
    return jnp.dot(a, b, preferred_element_type=F32)


def quantize(field):
    peak = jnp.max(jnp.abs(field), axis=2, keepdims=True)
    power = jnp.floor(4.0 * jnp.log2(32000.0 / jnp.maximum(peak, 1e-30)))
    return jnp.round(field * jnp.exp2(0.25 * power)).astype(jnp.int32), power + 512.0


def step_size(power):
    return jnp.exp2(0.25 * (512.0 - power))


def diagonal(blocks, lanes):
    shape = (blocks, PACK, lanes)
    return lax.broadcasted_iota(jnp.int32, shape, 1) == lax.broadcasted_iota(jnp.int32, shape, 2)


def lay_out(power, lanes):
    spread = jnp.where(diagonal(power.shape[0], lanes), power, 0.0)
    return jnp.sum(spread, axis=1, keepdims=True).astype(jnp.int32)


def stand_up(row):
    spread = jnp.where(diagonal(row.shape[0], row.shape[2]), row.astype(F32), 0.0)
    return jnp.sum(spread, axis=2, keepdims=True)


def pair(high, low):
    return (high << 16) | (low & 0xFFFF)


def first_of(word):
    return (word >> 16).astype(F32)


def second_of(word):
    return ((word << 16) >> 16).astype(F32)


def encode_one(field, target):
    steps, power = quantize(field)
    half = PACK // 2
    target[:, :half] = pair(steps, pltpu.roll(steps, half, 1))[:, :half]
    target[:, half:] = lay_out(power, field.shape[2])


def decode_one(source):
    half = PACK // 2
    words = source[:, :half]
    power = stand_up(source[:, half:])
    return jnp.concatenate([first_of(words), second_of(words)], axis=1) * step_size(power)


def encode_two(first, second, target):
    first_steps, first_power = quantize(first)
    second_steps, second_power = quantize(second)
    target[:, :PACK] = pair(first_steps, second_steps)
    target[:, PACK:] = lay_out(first_power + 1024.0 * second_power, first.shape[2])


def decode_two(source):
    words = source[:, :PACK]
    powers = stand_up(source[:, PACK:]).astype(jnp.int32)
    first_power = (powers & 1023).astype(F32)
    second_power = (powers >> 10).astype(F32)
    return first_of(words) * step_size(first_power), second_of(words) * step_size(second_power)


def adders(size):
    return [4, 2, 5, 3, 6, 0, 7, 1] if size == 8 else list(range(size))


def pick(values, index):
    return sum(jnp.where(index == place, int(value), 0) for place, value in enumerate(values))


def far_first(step, size):
    shift = lax.div(step + 1, 2)
    return lax.rem(size + size // 2 + jnp.where(lax.rem(step, 2) == 1, -shift, shift), size)


def stencil(field, taps):
    lanes = field.shape[2]
    lane = lax.broadcasted_iota(jnp.int32, field.shape, 2)
    edge = jnp.zeros((1,) + field.shape[1:], F32)
    turned = pltpu.roll(field, 1, 2)
    before = jnp.where(lane == 0, jnp.concatenate([edge, turned[:-1]], axis=0), turned)
    turned = pltpu.roll(field, lanes - 1, 2)
    after = jnp.where(lane == lanes - 1, jnp.concatenate([turned[1:], edge], axis=0), turned)
    return taps[0] * before + taps[1] * field + taps[2] * after


def kernel(
    tm_size,
    dp_size,
    ids_hbm,
    wave_hbm,
    cot_hbm,
    filt_hbm,
    taps_hbm,
    gain_hbm,
    speakers_hbm,
    table_hbm,
    layer_ref,
    gradw_ref,
    recv_g,
    ids,
    wave_ref,
    cot_ref,
    filt_ref,
    taps_ref,
    gain_ref,
    speakers,
    table,
    lh,
    ll,
    bh,
    bl,
    rh,
    rl,
    send_a,
    recv_a,
    send_f,
    recv_f,
    send_c,
    recv_c,
    send_r,
    recv_r,
    send_g,
    local_sem,
    send_sem,
    recv_sem,
    plane_sem,
):
    dp = lax.axis_index("dp")
    tm = lax.axis_index("tm")
    per = tm_size // dp_size
    place = lax.div(tm, dp_size)
    column_at = lax.rem(tm, dp_size)
    samples = wave_ref.shape[0]
    channels = wave_ref.shape[1]
    rows = tm_size * PACK

    pairs = [
        (wave_hbm, wave_ref),
        (cot_hbm, cot_ref),
        (filt_hbm, filt_ref),
        (table_hbm, table),
        (taps_hbm, taps_ref),
        (gain_hbm, gain_ref),
        (ids_hbm, ids),
        (speakers_hbm, speakers),
    ]
    loads = [
        pltpu.make_async_copy(source, target, local_sem.at[slot])
        for slot, (source, target) in enumerate(pairs)
    ]


    barrier = pltpu.get_barrier_semaphore()

    def tm_peer(step):
        far = far_first(lax.div(step, per), dp_size)
        across = far_first(lax.rem(step, per), per)
        return lax.rem(place + across, per) * dp_size + lax.rem(column_at + far, dp_size)

    def dp_peer(step):
        return lax.rem(dp + far_first(step, dp_size), dp_size)

    @pl.loop(0, tm_size - 1)
    def _(step):
        pl.semaphore_signal(barrier, inc=1, device_id=(dp, tm_peer(step)), device_id_type=MESH)

    @pl.loop(0, dp_size - 1)
    def _(step):
        pl.semaphore_signal(barrier, inc=1, device_id=(dp_peer(step), tm), device_id_type=MESH)

    for load in loads[:3]:
        load.start()

    def wait_bytes(like, sem):
        pltpu.make_async_copy(like, like, sem).wait()

    def exchange(source, target, which):
        @pl.loop(0, tm_size - 1)
        def _(step):
            peer = tm_peer(lax.rem(step + 15 * lax.rem(dp, 2), tm_size - 1))
            pltpu.make_async_remote_copy(
                src_ref=source.at[peer],
                dst_ref=target.at[tm],
                send_sem=send_sem.at[which],
                recv_sem=recv_sem.at[which],
                device_id=(dp, peer),
                device_id_type=MESH,
            ).start()

    def to_blocks(field):
        return field.reshape(tm_size, PACK, samples)

    loads[0].wait()
    wave_t = to_blocks(wave_ref[...].astype(F32).T)
    loads[1].wait()
    cot_t = to_blocks(cot_ref[...].astype(F32).T)
    send_a[...] = jnp.concatenate([wave_t, cot_t], axis=1).astype(BF16)
    pl.semaphore_wait(barrier, tm_size - 1 + dp_size - 1)
    exchange(send_a, recv_a, 0)
    recv_a[tm] = send_a[tm]

    adder = pick(adders(dp_size), lax.div(tm, per))
    share = pick(np.argsort(adders(dp_size)), dp)

    @pl.when(adder == dp)
    def _():
        @pl.loop(0, dp_size - 1)
        def _(step):
            pl.semaphore_signal(plane_sem, inc=1, device_id=(dp_peer(step), tm), device_id_type=MESH)

    for load in loads[3:]:
        load.start()
    for load in loads[3:]:
        load.wait()
    lh[...], ll[...] = split(table[:rows, :rows])
    bh[...], bl[...] = split(table[rows : 2 * rows, :rows])
    rh[...], rl[...] = split(table[2 * rows : 2 * rows + 2 * samples, : 2 * samples])
    tc = table[2 * rows + 2 * samples :, :samples]
    ts = table[2 * rows + 2 * samples :, samples : 2 * samples]
    loads[2].wait()
    encode_one(to_blocks(filt_ref[...].T), send_f)
    exchange(send_f, recv_f, 1)
    recv_f[tm] = send_f[tm]

    lane = lax.broadcasted_iota(jnp.int32, (PACK, channels), 1)
    row = lax.broadcasted_iota(jnp.int32, (PACK, channels), 0)
    mine = lane == tm * PACK + row

    def column(vector):
        return jnp.sum(jnp.where(mine, vector, 0.0), axis=1, keepdims=True)

    speaker = ids[0]
    group = speakers[lax.div(speaker, ROWS16)]
    picked = lax.broadcasted_iota(jnp.int32, (ROWS16, channels), 0) == lax.rem(speaker, ROWS16)
    speaker_row = jnp.sum(jnp.where(picked, group.astype(F32), 0.0), axis=0, keepdims=True)
    scale = column(speaker_row)
    taps = [column(taps_ref[place : place + 1, :]) for place in range(3)]
    gain = column(gain_ref[...])

    def left_mix(table_high, table_low, field):
        high, low = split(field)
        columns = field.shape[1]
        both = dot(table_high[...], jnp.concatenate([high, low], axis=1))
        return both[:, :columns] + (both[:, columns:] + dot(table_low[...], high))

    def right_mix(field):
        high, low = split(field)
        return dot(high, rh[...]) + (dot(high, rl[...]) + dot(low, rh[...]))

    def twiddle(real, imag):
        return real * tc + imag * ts, imag * tc - real * ts

    half_rows = (tm_size // 2 + 1) * PACK

    def forward(mixed):
        count = mixed.shape[1] // samples
        blank = jnp.zeros((PACK, samples), F32)
        turned = []
        for field in range(count):
            part = mixed[:, field * samples : (field + 1) * samples]
            imag = jnp.concatenate([blank, part[half_rows:], blank], axis=0)
            turned.append(jnp.concatenate(twiddle(part[:half_rows], imag), axis=1))
        result = right_mix(jnp.concatenate(turned, axis=0))
        parts = [result[field * half_rows : (field + 1) * half_rows] for field in range(count)]
        return [(part[:, :samples], part[:, samples:]) for part in parts]

    def backward(spectra):
        packed = [jnp.concatenate([real, -imag], axis=1) for real, imag in spectra]
        inner = right_mix(jnp.concatenate(packed, axis=0))
        turned = []
        for field in range(len(spectra)):
            part = inner[field * half_rows : (field + 1) * half_rows]
            real, imag = twiddle(part[:, :samples], part[:, samples:])
            turned.append(jnp.concatenate([real, imag[PACK:-PACK]], axis=0))
        return left_mix(bh, bl, jnp.concatenate(turned, axis=1))

    wait_bytes(recv_a.at[pl.ds(0, tm_size - 1)], recv_sem.at[0])
    both = recv_a[...].astype(F32)
    value = stencil(both[:, :PACK], taps) * scale
    grad = both[:, PACK:]
    value_high, value_low = split(value.reshape(rows, samples))
    high = jnp.concatenate([value_high, grad.reshape(rows, samples).astype(BF16)], axis=1)
    mixed = dot(lh[...], high) + dot(ll[...], high)
    mixed_value = mixed[:, :samples] + dot(lh[...], value_low)
    mixed = jnp.concatenate([mixed_value, mixed[:, samples:]], axis=1)
    (vr, vi), (gr, gi) = forward(mixed)
    send_r[...] = to_blocks(backward([(vr * gr + vi * gi, vr * gi - vi * gr)]))

    @pl.when(adder != dp)
    def _():
        pl.semaphore_wait(plane_sem, 1)

    slot = dp * per + lax.rem(tm, per)

    def send_partial(block):
        pltpu.make_async_remote_copy(
            src_ref=send_r.at[block],
            dst_ref=recv_r.at[slot],
            send_sem=send_sem.at[2],
            recv_sem=recv_sem.at[2],
            device_id=(adder, block),
            device_id_type=MESH,
        ).start()

    @pl.when(jnp.logical_not((tm == 0) & (adder == dp)))
    def _():
        send_partial(0)

    @pl.loop(0, tm_size)
    def _(step):
        block = lax.rem(step, per) * dp_size + lax.div(step, per)

        @pl.when((block != 0) & jnp.logical_not((block == tm) & (adder == dp)))
        def _():
            send_partial(block)

    @pl.when(adder == dp)
    def _():
        recv_r[slot] = send_r[tm]

    wait_bytes(recv_f.at[pl.ds(0, tm_size - 1)], recv_sem.at[1])
    ((fr, fi),) = forward(left_mix(lh, ll, decode_one(recv_f).reshape(rows, samples)))
    results = backward(
        [
            (vr * fr - vi * fi, vr * fi + vi * fr),
            (gr * fr + gi * fi, gi * fr - gr * fi),
        ]
    )
    convolved, correlated = results[:, :samples], results[:, samples:]
    layer = to_blocks(convolved) + gain * value
    middle = (to_blocks(correlated) + gain * grad) * scale
    encode_two(layer, stencil(middle, taps[::-1]), send_c)
    @pl.loop(0, tm_size)
    def _(step):
        peer = lax.rem(place + far_first(lax.rem(step, per), per), per) * dp_size + lax.div(step, per)

        @pl.when(peer != tm)
        def _():
            pltpu.make_async_remote_copy(
                src_ref=send_c.at[peer],
                dst_ref=recv_c.at[tm],
                send_sem=send_sem.at[3],
                recv_sem=recv_sem.at[3],
                device_id=(dp, peer),
                device_id_type=MESH,
            ).start()

    recv_c[tm] = send_c[tm]

    @pl.when(adder == dp)
    def _():
        wait_bytes(recv_r.at[pl.ds(0, tm_size - 1)], recv_sem.at[2])

    @pl.when(adder != dp)
    def _():
        wait_bytes(recv_r, recv_sem.at[2])

    send_g[...] = jnp.sum(recv_r[...].reshape(dp_size, per, PACK, samples), axis=0)
    summed = recv_g.at[pl.ds(share * per, per)]

    @pl.loop(0, dp_size - 1)
    def _(step):
        pltpu.make_async_remote_copy(
            src_ref=send_g,
            dst_ref=summed,
            send_sem=send_sem.at[4],
            recv_sem=recv_sem.at[4],
            device_id=(dp_peer(dp_size - 2 - step), tm),
            device_id_type=MESH,
        ).start()

    own_g = pltpu.make_async_copy(send_g, summed, local_sem.at[9])
    own_g.start()
    wait_bytes(recv_c.at[pl.ds(0, tm_size - 1)], recv_sem.at[3])
    layer, gradw = decode_two(recv_c)
    layer_ref[...] = layer.reshape(channels, samples).T
    gradw_ref[...] = gradw.reshape(channels, samples).T
    wait_bytes(send_a.at[pl.ds(0, tm_size - 1)], send_sem.at[0])
    wait_bytes(send_f.at[pl.ds(0, tm_size - 1)], send_sem.at[1])
    wait_bytes(send_c.at[pl.ds(0, tm_size - 1)], send_sem.at[3])

    @pl.when(adder == dp)
    def _():
        wait_bytes(send_r.at[pl.ds(0, tm_size - 1)], send_sem.at[2])

    @pl.when(adder != dp)
    def _():
        wait_bytes(send_r, send_sem.at[2])

    wait_bytes(recv_g.at[pl.ds(0, tm_size - per)], send_sem.at[4])
    own_g.wait()
    wait_bytes(recv_g.at[pl.ds(0, tm_size - per)], recv_sem.at[4])


def finish(layer_in, gradw_in, third, layer_hbm, gradw_hbm, fgrad_hbm, turned, store_sem):
    channels, samples = turned.shape[1], turned.shape[0]
    stores = [
        pltpu.make_async_copy(layer_in, layer_hbm, store_sem.at[0]),
        pltpu.make_async_copy(gradw_in, gradw_hbm, store_sem.at[1]),
        pltpu.make_async_copy(turned, fgrad_hbm, store_sem.at[2]),
    ]
    stores[0].start()
    stores[1].start()
    turned[...] = third[...].reshape(channels, samples).T
    stores[2].start()
    for store in stores:
        store.wait()


def local(waveform, speaker_ids, speaker_table, stencil_taps, skip_gain, filters, cotangent):
    tm_size, dp_size = lax.axis_size("tm"), lax.axis_size("dp")
    samples, channels = filters.shape
    per = tm_size // dp_size
    rows = tm_size * PACK
    table = make_table(tm_size, samples)
    anywhere = pl.BlockSpec(memory_space=pl.ANY)
    vmem = pl.BlockSpec(memory_space=pltpu.VMEM)
    block = jax.ShapeDtypeStruct((samples, channels), F32)
    pieces = jax.ShapeDtypeStruct((tm_size, PACK, samples), F32)
    received = pl.pallas_call(
        functools.partial(kernel, tm_size, dp_size),
        out_shape=[pltpu.VMEM(block.shape, F32)] * 2 + [pltpu.VMEM(pieces.shape, F32)],
        in_specs=[anywhere] * 8,
        out_specs=[vmem] * 3,
        scratch_shapes=[
            pltpu.SMEM((1,), jnp.int32),
            pltpu.VMEM((samples, channels), BF16),
            pltpu.VMEM((samples, channels), BF16),
            pltpu.VMEM((samples, channels), F32),
            pltpu.VMEM(stencil_taps.shape, F32),
            pltpu.VMEM((1, channels), F32),
            pltpu.VMEM((speaker_table.shape[0] // ROWS16, ROWS16, channels), BF16),
            pltpu.VMEM(table.shape, F32),
            *[pltpu.VMEM((rows, rows), BF16)] * 4,
            pltpu.VMEM((2 * samples, 2 * samples), BF16),
            pltpu.VMEM((2 * samples, 2 * samples), BF16),
            pltpu.VMEM((tm_size, 2 * PACK, samples), BF16),
            pltpu.VMEM((tm_size, 2 * PACK, samples), BF16),
            pltpu.VMEM((tm_size, PACK // 2 + 1, samples), jnp.int32),
            pltpu.VMEM((tm_size, PACK // 2 + 1, samples), jnp.int32),
            pltpu.VMEM((tm_size, PACK + 1, samples), jnp.int32),
            pltpu.VMEM((tm_size, PACK + 1, samples), jnp.int32),
            pltpu.VMEM((tm_size, PACK, samples), F32),
            pltpu.VMEM((tm_size, PACK, samples), F32),
            pltpu.VMEM((per, PACK, samples), F32),
            pltpu.SemaphoreType.DMA((11,)),
            pltpu.SemaphoreType.DMA((6,)),
            pltpu.SemaphoreType.DMA((6,)),
            pltpu.SemaphoreType.REGULAR,
        ],
        compiler_params=pltpu.CompilerParams(
            collective_id=0, has_side_effects=True, vmem_limit_bytes=32 * 1024 * 1024
        ),
    )(
        speaker_ids,
        *[
            pltpu.with_memory_space_constraint(operand, pltpu.HBM)
            for operand in (
                waveform[0],
                cotangent[0],
                filters,
                stencil_taps,
                skip_gain[None],
                speaker_table.reshape(-1, ROWS16, channels),
                jnp.asarray(table),
            )
        ]
    )
    layer_out, grad_waveform, filter_grad = pl.pallas_call(
        finish,
        out_shape=[block, block, block],
        in_specs=[vmem] * 3,
        out_specs=[anywhere] * 3,
        scratch_shapes=[
            pltpu.VMEM((samples, channels), F32),
            pltpu.SemaphoreType.DMA((3,)),
        ],
        compiler_params=pltpu.CompilerParams(vmem_limit_bytes=16 * 1024 * 1024),
    )(*received)
    return layer_out[None], grad_waveform[None], filter_grad


def solution(mesh):
    return jax.shard_map(
        local,
        mesh=mesh,
        in_specs=(P("dp", "tm", None), P("dp"), P(), P(), P(), P("tm", None), P("dp", "tm", None)),
        out_specs=(P("dp", "tm", None), P("dp", "tm", None), P("tm", None)),
        check_vma=False,
    )
```

```python
import functools
import math

import jax
import jax.numpy as jnp
import numpy as np
from jax import lax
from jax.experimental import pallas as pl
from jax.experimental.pallas import tpu as pltpu
from jax.sharding import PartitionSpec as P

MESH = pl.DeviceIdType.MESH
F32 = jnp.float32
BF16 = jnp.bfloat16
PACK = 8
ROWS16 = 16


def make_table(blocks, samples):
    total = blocks * samples
    spread = np.eye(PACK)
    block = np.arange(blocks)
    low = np.arange(blocks // 2 + 1)
    angle = 2.0 * math.pi / blocks * (np.outer(low, block) % blocks)
    forward = np.concatenate([np.cos(angle), -np.sin(angle)[1:-1]])
    weight = np.where((low == 0) | (low == blocks // 2), 1.0, 2.0)[:, None] / total
    backward = np.concatenate([weight * np.cos(angle), (weight * np.sin(angle))[1:-1]]).T
    inner = np.arange(samples)
    angle = 2.0 * math.pi / samples * (np.outer(inner, inner) % samples)
    right = np.block([[np.cos(angle), -np.sin(angle)], [np.sin(angle), np.cos(angle)]])
    turn = np.repeat(2.0 * math.pi / total * np.outer(low, inner), PACK, axis=0)
    turn = np.concatenate([np.cos(turn), np.sin(turn)], axis=1)
    parts = [np.kron(forward, spread), np.kron(backward, spread), right, turn]
    wide = max(part.shape[1] for part in parts)
    parts = [np.pad(part, ((0, 0), (0, wide - part.shape[1]))) for part in parts]
    return np.concatenate(parts).astype(np.float32)


def split(array):
    high = array.astype(BF16)
    return high, (array - high.astype(F32)).astype(BF16)


def dot(a, b):
    return jnp.dot(a, b, preferred_element_type=F32)


def quantize(field):
    peak = jnp.max(jnp.abs(field), axis=2, keepdims=True)
    power = jnp.floor(4.0 * jnp.log2(32000.0 / jnp.maximum(peak, 1e-30)))
    return jnp.round(field * jnp.exp2(0.25 * power)).astype(jnp.int32), power + 512.0


def step_size(power):
    return jnp.exp2(0.25 * (512.0 - power))


def diagonal(blocks, lanes):
    shape = (blocks, PACK, lanes)
    return lax.broadcasted_iota(jnp.int32, shape, 1) == lax.broadcasted_iota(jnp.int32, shape, 2)


def lay_out(power, lanes):
    spread = jnp.where(diagonal(power.shape[0], lanes), power, 0.0)
    return jnp.sum(spread, axis=1, keepdims=True).astype(jnp.int32)


def stand_up(row):
    spread = jnp.where(diagonal(row.shape[0], row.shape[2]), row.astype(F32), 0.0)
    return jnp.sum(spread, axis=2, keepdims=True)


def pair(high, low):
    return (high << 16) | (low & 0xFFFF)


def first_of(word):
    return (word >> 16).astype(F32)


def second_of(word):
    return ((word << 16) >> 16).astype(F32)


def encode_one(field, target):
    steps, power = quantize(field)
    half = PACK // 2
    target[:, :half] = pair(steps, pltpu.roll(steps, half, 1))[:, :half]
    target[:, half:] = lay_out(power, field.shape[2])


def decode_one(source):
    half = PACK // 2
    words = source[:, :half]
    power = stand_up(source[:, half:])
    return jnp.concatenate([first_of(words), second_of(words)], axis=1) * step_size(power)


def encode_two(first, second, target):
    first_steps, first_power = quantize(first)
    second_steps, second_power = quantize(second)
    target[:, :PACK] = pair(first_steps, second_steps)
    target[:, PACK:] = lay_out(first_power + 1024.0 * second_power, first.shape[2])


def decode_two(source):
    words = source[:, :PACK]
    powers = stand_up(source[:, PACK:]).astype(jnp.int32)
    first_power = (powers & 1023).astype(F32)
    second_power = (powers >> 10).astype(F32)
    return first_of(words) * step_size(first_power), second_of(words) * step_size(second_power)


def adders(size):
    return [4, 2, 5, 3, 6, 0, 7, 1] if size == 8 else list(range(size))


def pick(values, index):
    return sum(jnp.where(index == place, int(value), 0) for place, value in enumerate(values))


def far_first(step, size):
    shift = lax.div(step + 1, 2)
    return lax.rem(size + size // 2 + jnp.where(lax.rem(step, 2) == 1, -shift, shift), size)


def stencil(field, taps):
    lanes = field.shape[2]
    lane = lax.broadcasted_iota(jnp.int32, field.shape, 2)
    edge = jnp.zeros((1,) + field.shape[1:], F32)
    turned = pltpu.roll(field, 1, 2)
    before = jnp.where(lane == 0, jnp.concatenate([edge, turned[:-1]], axis=0), turned)
    turned = pltpu.roll(field, lanes - 1, 2)
    after = jnp.where(lane == lanes - 1, jnp.concatenate([turned[1:], edge], axis=0), turned)
    return taps[0] * before + taps[1] * field + taps[2] * after


def kernel(
    tm_size,
    dp_size,
    ids_hbm,
    wave_hbm,
    cot_hbm,
    filt_hbm,
    taps_hbm,
    gain_hbm,
    speakers_hbm,
    table_hbm,
    layer_ref,
    gradw_ref,
    recv_g,
    ids,
    wave_ref,
    cot_ref,
    filt_ref,
    taps_ref,
    gain_ref,
    speakers,
    table,
    lh,
    ll,
    bh,
    bl,
    rh,
    rl,
    send_a,
    recv_a,
    send_f,
    recv_f,
    send_c,
    recv_c,
    send_r,
    recv_r,
    send_g,
    local_sem,
    send_sem,
    recv_sem,
    plane_sem,
):
    dp = lax.axis_index("dp")
    tm = lax.axis_index("tm")
    per = tm_size // dp_size
    place = lax.div(tm, dp_size)
    column_at = lax.rem(tm, dp_size)
    samples = wave_ref.shape[0]
    channels = wave_ref.shape[1]
    rows = tm_size * PACK

    pairs = [
        (wave_hbm, wave_ref),
        (cot_hbm, cot_ref),
        (filt_hbm, filt_ref),
        (table_hbm, table),
        (taps_hbm, taps_ref),
        (gain_hbm, gain_ref),
        (ids_hbm, ids),
        (speakers_hbm, speakers),
    ]
    loads = [
        pltpu.make_async_copy(source, target, local_sem.at[slot])
        for slot, (source, target) in enumerate(pairs)
    ]

    for load in loads[:3]:
        load.start()

    barrier = pltpu.get_barrier_semaphore()

    def tm_peer(step):
        far = far_first(lax.div(step, per), dp_size)
        across = far_first(lax.rem(step, per), per)
        return lax.rem(place + across, per) * dp_size + lax.rem(column_at + far, dp_size)

    def dp_peer(step):
        return lax.rem(dp + far_first(step, dp_size), dp_size)

    @pl.loop(0, tm_size - 1)
    def _(step):
        pl.semaphore_signal(barrier, inc=1, device_id=(dp, tm_peer(step)), device_id_type=MESH)

    @pl.loop(0, dp_size - 1)
    def _(step):
        pl.semaphore_signal(barrier, inc=1, device_id=(dp_peer(step), tm), device_id_type=MESH)

    def wait_bytes(like, sem):
        pltpu.make_async_copy(like, like, sem).wait()

    def exchange(source, target, which):
        @pl.loop(0, tm_size - 1)
        def _(step):
            peer = tm_peer(lax.rem(step + 15 * lax.rem(dp, 2), tm_size - 1))
            pltpu.make_async_remote_copy(
                src_ref=source.at[peer],
                dst_ref=target.at[tm],
                send_sem=send_sem.at[which],
                recv_sem=recv_sem.at[which],
                device_id=(dp, peer),
                device_id_type=MESH,
            ).start()

    def to_blocks(field):
        return field.reshape(tm_size, PACK, samples)

    loads[0].wait()
    wave_t = to_blocks(wave_ref[...].astype(F32).T)
    loads[1].wait()
    cot_t = to_blocks(cot_ref[...].astype(F32).T)
    send_a[...] = jnp.concatenate([wave_t, cot_t], axis=1).astype(BF16)
    pl.semaphore_wait(barrier, tm_size - 1 + dp_size - 1)
    exchange(send_a, recv_a, 0)
    recv_a[tm] = send_a[tm]

    adder = pick(adders(dp_size), lax.div(tm, per))
    share = pick(np.argsort(adders(dp_size)), dp)

    @pl.when(adder == dp)
    def _():
        @pl.loop(0, dp_size - 1)
        def _(step):
            pl.semaphore_signal(plane_sem, inc=1, device_id=(dp_peer(step), tm), device_id_type=MESH)

    for load in loads[3:]:
        load.start()
    for load in loads[3:]:
        load.wait()
    lh[...], ll[...] = split(table[:rows, :rows])
    bh[...], bl[...] = split(table[rows : 2 * rows, :rows])
    rh[...], rl[...] = split(table[2 * rows : 2 * rows + 2 * samples, : 2 * samples])
    tc = table[2 * rows + 2 * samples :, :samples]
    ts = table[2 * rows + 2 * samples :, samples : 2 * samples]
    loads[2].wait()
    encode_one(to_blocks(filt_ref[...].T), send_f)
    exchange(send_f, recv_f, 1)
    recv_f[tm] = send_f[tm]

    lane = lax.broadcasted_iota(jnp.int32, (PACK, channels), 1)
    row = lax.broadcasted_iota(jnp.int32, (PACK, channels), 0)
    mine = lane == tm * PACK + row

    def column(vector):
        return jnp.sum(jnp.where(mine, vector, 0.0), axis=1, keepdims=True)

    speaker = ids[0]
    group = speakers[lax.div(speaker, ROWS16)]
    picked = lax.broadcasted_iota(jnp.int32, (ROWS16, channels), 0) == lax.rem(speaker, ROWS16)
    speaker_row = jnp.sum(jnp.where(picked, group.astype(F32), 0.0), axis=0, keepdims=True)
    scale = column(speaker_row)
    taps = [column(taps_ref[place : place + 1, :]) for place in range(3)]
    gain = column(gain_ref[...])

    def left_mix(table_high, table_low, field):
        high, low = split(field)
        columns = field.shape[1]
        both = dot(table_high[...], jnp.concatenate([high, low], axis=1))
        return both[:, :columns] + (both[:, columns:] + dot(table_low[...], high))

    def right_mix(field):
        high, low = split(field)
        return dot(high, rh[...]) + (dot(high, rl[...]) + dot(low, rh[...]))

    def twiddle(real, imag):
        return real * tc + imag * ts, imag * tc - real * ts

    half_rows = (tm_size // 2 + 1) * PACK

    def forward(mixed):
        count = mixed.shape[1] // samples
        blank = jnp.zeros((PACK, samples), F32)
        turned = []
        for field in range(count):
            part = mixed[:, field * samples : (field + 1) * samples]
            imag = jnp.concatenate([blank, part[half_rows:], blank], axis=0)
            turned.append(jnp.concatenate(twiddle(part[:half_rows], imag), axis=1))
        result = right_mix(jnp.concatenate(turned, axis=0))
        parts = [result[field * half_rows : (field + 1) * half_rows] for field in range(count)]
        return [(part[:, :samples], part[:, samples:]) for part in parts]

    def backward(spectra):
        packed = [jnp.concatenate([real, -imag], axis=1) for real, imag in spectra]
        inner = right_mix(jnp.concatenate(packed, axis=0))
        turned = []
        for field in range(len(spectra)):
            part = inner[field * half_rows : (field + 1) * half_rows]
            real, imag = twiddle(part[:, :samples], part[:, samples:])
            turned.append(jnp.concatenate([real, imag[PACK:-PACK]], axis=0))
        return left_mix(bh, bl, jnp.concatenate(turned, axis=1))

    wait_bytes(recv_a.at[pl.ds(0, tm_size - 1)], recv_sem.at[0])
    both = recv_a[...].astype(F32)
    value = stencil(both[:, :PACK], taps) * scale
    grad = both[:, PACK:]
    value_high, value_low = split(value.reshape(rows, samples))
    high = jnp.concatenate([value_high, grad.reshape(rows, samples).astype(BF16)], axis=1)
    mixed = dot(lh[...], high) + dot(ll[...], high)
    mixed_value = mixed[:, :samples] + dot(lh[...], value_low)
    mixed = jnp.concatenate([mixed_value, mixed[:, samples:]], axis=1)
    (vr, vi), (gr, gi) = forward(mixed)
    send_r[...] = to_blocks(backward([(vr * gr + vi * gi, vr * gi - vi * gr)]))

    @pl.when(adder != dp)
    def _():
        pl.semaphore_wait(plane_sem, 1)

    slot = dp * per + lax.rem(tm, per)

    def send_partial(block):
        pltpu.make_async_remote_copy(
            src_ref=send_r.at[block],
            dst_ref=recv_r.at[slot],
            send_sem=send_sem.at[2],
            recv_sem=recv_sem.at[2],
            device_id=(adder, block),
            device_id_type=MESH,
        ).start()

    @pl.when(jnp.logical_not((tm == 0) & (adder == dp)))
    def _():
        send_partial(0)

    @pl.loop(0, tm_size)
    def _(step):
        block = lax.rem(step, per) * dp_size + lax.div(step, per)

        @pl.when((block != 0) & jnp.logical_not((block == tm) & (adder == dp)))
        def _():
            send_partial(block)

    @pl.when(adder == dp)
    def _():
        recv_r[slot] = send_r[tm]

    wait_bytes(recv_f.at[pl.ds(0, tm_size - 1)], recv_sem.at[1])
    ((fr, fi),) = forward(left_mix(lh, ll, decode_one(recv_f).reshape(rows, samples)))
    results = backward(
        [
            (vr * fr - vi * fi, vr * fi + vi * fr),
            (gr * fr + gi * fi, gi * fr - gr * fi),
        ]
    )
    convolved, correlated = results[:, :samples], results[:, samples:]
    layer = to_blocks(convolved) + gain * value
    middle = (to_blocks(correlated) + gain * grad) * scale
    encode_two(layer, stencil(middle, taps[::-1]), send_c)
    exchange(send_c, recv_c, 3)
    recv_c[tm] = send_c[tm]

    @pl.when(adder == dp)
    def _():
        wait_bytes(recv_r.at[pl.ds(0, tm_size - 1)], recv_sem.at[2])

    @pl.when(adder != dp)
    def _():
        wait_bytes(recv_r, recv_sem.at[2])

    send_g[...] = jnp.sum(recv_r[...].reshape(dp_size, per, PACK, samples), axis=0)
    summed = recv_g.at[pl.ds(share * per, per)]

    @pl.loop(0, dp_size - 1)
    def _(step):
        pltpu.make_async_remote_copy(
            src_ref=send_g,
            dst_ref=summed,
            send_sem=send_sem.at[4],
            recv_sem=recv_sem.at[4],
            device_id=(dp_peer(step), tm),
            device_id_type=MESH,
        ).start()

    own_g = pltpu.make_async_copy(send_g, summed, local_sem.at[9])
    own_g.start()
    wait_bytes(recv_c.at[pl.ds(0, tm_size - 1)], recv_sem.at[3])
    layer, gradw = decode_two(recv_c)
    layer_ref[...] = layer.reshape(channels, samples).T
    gradw_ref[...] = gradw.reshape(channels, samples).T
    wait_bytes(send_a.at[pl.ds(0, tm_size - 1)], send_sem.at[0])
    wait_bytes(send_f.at[pl.ds(0, tm_size - 1)], send_sem.at[1])
    wait_bytes(send_c.at[pl.ds(0, tm_size - 1)], send_sem.at[3])

    @pl.when(adder == dp)
    def _():
        wait_bytes(send_r.at[pl.ds(0, tm_size - 1)], send_sem.at[2])

    @pl.when(adder != dp)
    def _():
        wait_bytes(send_r, send_sem.at[2])

    wait_bytes(recv_g.at[pl.ds(0, tm_size - per)], send_sem.at[4])
    own_g.wait()
    wait_bytes(recv_g.at[pl.ds(0, tm_size - per)], recv_sem.at[4])


def finish(layer_in, gradw_in, third, layer_hbm, gradw_hbm, fgrad_hbm, turned, store_sem):
    channels, samples = turned.shape[1], turned.shape[0]
    stores = [
        pltpu.make_async_copy(layer_in, layer_hbm, store_sem.at[0]),
        pltpu.make_async_copy(gradw_in, gradw_hbm, store_sem.at[1]),
        pltpu.make_async_copy(turned, fgrad_hbm, store_sem.at[2]),
    ]
    stores[0].start()
    stores[1].start()
    turned[...] = third[...].reshape(channels, samples).T
    stores[2].start()
    for store in stores:
        store.wait()


def local(waveform, speaker_ids, speaker_table, stencil_taps, skip_gain, filters, cotangent):
    tm_size, dp_size = lax.axis_size("tm"), lax.axis_size("dp")
    samples, channels = filters.shape
    per = tm_size // dp_size
    rows = tm_size * PACK
    table = make_table(tm_size, samples)
    anywhere = pl.BlockSpec(memory_space=pl.ANY)
    vmem = pl.BlockSpec(memory_space=pltpu.VMEM)
    block = jax.ShapeDtypeStruct((samples, channels), F32)
    pieces = jax.ShapeDtypeStruct((tm_size, PACK, samples), F32)
    received = pl.pallas_call(
        functools.partial(kernel, tm_size, dp_size),
        out_shape=[pltpu.VMEM(block.shape, F32)] * 2 + [pltpu.VMEM(pieces.shape, F32)],
        in_specs=[anywhere] * 8,
        out_specs=[vmem] * 3,
        scratch_shapes=[
            pltpu.SMEM((1,), jnp.int32),
            pltpu.VMEM((samples, channels), BF16),
            pltpu.VMEM((samples, channels), BF16),
            pltpu.VMEM((samples, channels), F32),
            pltpu.VMEM(stencil_taps.shape, F32),
            pltpu.VMEM((1, channels), F32),
            pltpu.VMEM((speaker_table.shape[0] // ROWS16, ROWS16, channels), BF16),
            pltpu.VMEM(table.shape, F32),
            *[pltpu.VMEM((rows, rows), BF16)] * 4,
            pltpu.VMEM((2 * samples, 2 * samples), BF16),
            pltpu.VMEM((2 * samples, 2 * samples), BF16),
            pltpu.VMEM((tm_size, 2 * PACK, samples), BF16),
            pltpu.VMEM((tm_size, 2 * PACK, samples), BF16),
            pltpu.VMEM((tm_size, PACK // 2 + 1, samples), jnp.int32),
            pltpu.VMEM((tm_size, PACK // 2 + 1, samples), jnp.int32),
            pltpu.VMEM((tm_size, PACK + 1, samples), jnp.int32),
            pltpu.VMEM((tm_size, PACK + 1, samples), jnp.int32),
            pltpu.VMEM((tm_size, PACK, samples), F32),
            pltpu.VMEM((tm_size, PACK, samples), F32),
            pltpu.VMEM((per, PACK, samples), F32),
            pltpu.SemaphoreType.DMA((11,)),
            pltpu.SemaphoreType.DMA((6,)),
            pltpu.SemaphoreType.DMA((6,)),
            pltpu.SemaphoreType.REGULAR,
        ],
        compiler_params=pltpu.CompilerParams(
            collective_id=0, has_side_effects=True, vmem_limit_bytes=32 * 1024 * 1024
        ),
    )(
        speaker_ids,
        *[
            pltpu.with_memory_space_constraint(operand, pltpu.HBM)
            for operand in (
                waveform[0],
                cotangent[0],
                filters,
                stencil_taps,
                skip_gain[None],
                speaker_table.reshape(-1, ROWS16, channels),
                jnp.asarray(table),
            )
        ]
    )
    layer_out, grad_waveform, filter_grad = pl.pallas_call(
        finish,
        out_shape=[block, block, block],
        in_specs=[vmem] * 3,
        out_specs=[anywhere] * 3,
        scratch_shapes=[
            pltpu.VMEM((samples, channels), F32),
            pltpu.SemaphoreType.DMA((3,)),
        ],
        compiler_params=pltpu.CompilerParams(vmem_limit_bytes=16 * 1024 * 1024),
    )(*received)
    return layer_out[None], grad_waveform[None], filter_grad


def solution(mesh):
    return jax.shard_map(
        local,
        mesh=mesh,
        in_specs=(P("dp", "tm", None), P("dp"), P(), P(), P(), P("tm", None), P("dp", "tm", None)),
        out_specs=(P("dp", "tm", None), P("dp", "tm", None), P("tm", None)),
        check_vma=False,
    )
```
